256 devices in a mesh: expert: 64 (over z, x, core), tensor: 4 (over y).
Axes of the slice: x: 4, y: 4, z: 8, core: 2. Of those that a mesh axis runs over, the one named last changes fastest.
Arguments:
- tokens: bfloat16 [8192, 3584], P('expert', 'tensor'), may hold values from -6 to 6
- tangents: bfloat16 [8192, 3584], P('expert', 'tensor'), may hold values from -6 to 6
- routes: int32 [8192, 8], P('expert'), may hold values from 0 to 63, all different within a row; in each aligned block of 128 rows (0 to 127, 128 to 255, ...) at most 20 rows name the same one
- gates: float32 [8192, 8], P('expert'), may hold values from 0.02 to 0.6
- gate_weight: bfloat16 [64, 3584, 1024], P('expert', None, 'tensor'), may hold values from -0.09375 to 0.09375
- up_weight: bfloat16 [64, 3584, 1024], P('expert', None, 'tensor'), may hold values from -0.09375 to 0.09375
- down_weight: bfloat16 [64, 1024, 3584], P('expert', 'tensor'), may hold values from -0.1875 to 0.1875
- readout: bfloat16 [3584], replicated, may hold values from -6 to 6
Outputs:
- curvature: bfloat16 [8192, 3584], P('expert', 'tensor')
The draws below stay inside these ranges and needn't reach their ends.
Inputs may be any that keep to these rules, and one draw needn't show every extreme that they name: `routes`: A token's 8 experts differ. Among the tokens of one index of expert (aligned blocks of 128 tokens) no expert is named more than 20 times, a bound that some block reaches.
All inputs are finite; a program needn't handle non-finite values.
Results may differ from the reference program's by a relative error of at most 0.012.
Values may be sent and summed in bfloat16 or wider, within the bound.
A program may use at most 128 MiB of HBM per device.

```python
import math
import jax
import jax.numpy as jnp
import numpy as np
from jax import lax

D = 3584
FF = 1024
TOP = 8
TOK_DEV = 128
EXPERTS = 64
MOST = 20
TOKENS = 8192
N_EXPERT = 64
N_TENSOR = 4


def shard_levels(key, shape, split, low, largest):
    gain, own = 1.0, jax.random.fold_in(key, 6)
    for dim, blocks in split:
        steps = jnp.exp(jax.random.uniform(jax.random.fold_in(own, dim), (blocks,), jnp.float32, low / len(split), largest / len(split)))
        gain = gain * jnp.repeat(steps, shape[dim] // blocks).reshape([-1 if axis == dim else 1 for axis in range(len(shape))])
    return gain


def assign_block(key, own, number, rows, count, top, limit, lean):
    ranking = jax.random.permutation(key, count)
    crowded, common = load_shares(count, rows * top, limit, lean, True), load_shares(count, rows * top, limit, lean, False)
    places = jnp.arange(count)

    def named(lengths, turn):
        used = int((lengths > 0).sum())
        fixed = max(1, used // 4)
        shifted = fixed + (places - fixed + turn * (used - fixed)) % max(1, count - fixed)
        return jnp.zeros((count,), jnp.int32).at[ranking[jnp.where(places < fixed, places, shifted)]].set(jnp.asarray(lengths, jnp.int32))

    lengths = jnp.where(number % 4 == 0, named(crowded, number // 4), named(common, number - number // 4 - 1))
    mixed = jax.random.permutation(jax.random.fold_in(own, 3), count)
    source_of, sink = mixed[0:count // 2 * 2:2], mixed[1:count // 2 * 2:2]
    margin = jnp.minimum(lengths[source_of] - 1, limit - lengths[sink]) // 2
    margin = jnp.where((source_of == ranking[0]) | (sink == ranking[0]) | (lengths[sink] == 0), 0, jnp.maximum(margin, 0))
    shifted = jax.random.randint(jax.random.fold_in(own, 4), (count // 2,), 0, 1 << 20) % (margin + 1)
    lengths = lengths.at[source_of].add(-shifted).at[sink].add(shifted)
    members = jnp.searchsorted(jnp.cumsum(lengths), jnp.arange(rows * top), side="right").astype(jnp.int32)
    grid = members.reshape(top, rows).T
    grid = grid[jax.random.permutation(jax.random.fold_in(own, 1), rows)]
    turn = jax.random.randint(jax.random.fold_in(own, 2), (rows, 1), 0, top)
    return jnp.take_along_axis(grid, (jnp.arange(top)[None, :] + turn) % top, axis=1)


def load_shares(count, total, most, slope, full):
    weights = [(1 << 20) // math.isqrt(standing ** slope) + 1 for standing in range(1, count + 1)]
    largest = most if full else min(most, max(-(-total // count), total * weights[0] // sum(weights)))
    least = 1 if total - largest >= count - 1 else 0
    given, surplus = [largest] + [least] * (count - 1), total - largest - least * (count - 1)
    while surplus > 0:
        candidates = [i for i in range(1, count) if given[i] < largest] or [i for i in range(1, count) if given[i] < most]
        pool, remaining = sum([weights[i] for i in candidates]), surplus
        for i in candidates:
            addition = min(most - given[i], max(1, remaining * weights[i] // pool), surplus)
            given[i] = given[i] + addition
            surplus = surplus - addition
    return np.array(given)


def bell_draw(stream_key, extent, scale, limit, pieces=(), kind=jnp.bfloat16):
    values = scale * jax.random.normal(stream_key, extent, jnp.float32)
    if pieces:
        values = values * shard_levels(stream_key, extent, pieces, -0.22, 0.18)
    return jnp.clip(values, -limit, limit).astype(kind)


def setup_inputs(seed: int = 0) -> dict:
    key_of = jax.random.split(jax.random.key(seed), 9)
    tokens = bell_draw(key_of[0], (TOKENS, D), 1.0, 6.0, ((0, 64), (1, 4)))
    tangents = bell_draw(key_of[1], (TOKENS, D), 1.0, 6.0, ((0, 64), (1, 4)))
    routes_keys = jax.random.split(jax.random.fold_in(key_of[2], 1), TOKENS // TOK_DEV)
    routes_turns = jax.random.permutation(jax.random.fold_in(key_of[2], 3), TOKENS // TOK_DEV)
    routes = jax.vmap(lambda own, number: assign_block(jax.random.fold_in(key_of[2], 2), own, number, TOK_DEV, EXPERTS, TOP, MOST, 2))(routes_keys, routes_turns).reshape((TOKENS, TOP))
    gates = jnp.clip(jnp.exp(math.log(0.6) - 3.4011974 * jax.random.uniform(key_of[3], (TOKENS, TOP), jnp.float32) ** shard_levels(key_of[3], (TOKENS, TOP), ((0, 64),), -0.2, 0.2)), 0.02, 0.6)
    gate_weight = bell_draw(key_of[4], (EXPERTS, D, FF), D ** -0.5, 0.09375, ((0, 64), (2, 4)))
    up_weight = bell_draw(key_of[5], (EXPERTS, D, FF), D ** -0.5, 0.09375, ((0, 64), (2, 4)))
    down_weight = bell_draw(key_of[6], (EXPERTS, FF, D), FF ** -0.5, 0.1875, ((0, 64), (1, 4)))
    readout = bell_draw(key_of[7], (D,), 1.0, 6.0)
    return dict(tokens=tokens, tangents=tangents, routes=routes, gates=gates, gate_weight=gate_weight, up_weight=up_weight, down_weight=down_weight, readout=readout)


def coefficients(x_rows, v_rows, w_gate, w_up, w_down, readout):
    back = jnp.dot(w_down, readout, preferred_element_type=jnp.float32)
    h = jnp.dot(x_rows, w_gate, preferred_element_type=jnp.float32)
    u = jnp.dot(x_rows, w_up, preferred_element_type=jnp.float32)
    dh = jnp.dot(v_rows, w_gate, preferred_element_type=jnp.float32)
    du = jnp.dot(v_rows, w_up, preferred_element_type=jnp.float32)
    sig = jax.nn.sigmoid(h)
    first = sig * (1.0 + h * (1.0 - sig))
    second = sig * (1.0 - sig) * (2.0 + h * (1.0 - 2.0 * sig))
    coef_gate = (back[None, :] * (du * first + u * second * dh)).astype(jnp.bfloat16)
    coef_up = (back[None, :] * first * dh).astype(jnp.bfloat16)
    return coef_gate, coef_up


def reference(tokens, tangents, routes, gates, gate_weight, up_weight, down_weight, readout):
    capacity = N_EXPERT * MOST
    block_width = FF // N_TENSOR
    flat_ids = routes.reshape(-1).astype(jnp.int32)
    flat_gates = gates.reshape(-1)
    order = jnp.argsort(flat_ids, stable=True).astype(jnp.int32)
    counts = jnp.bincount(flat_ids, length=EXPERTS).astype(jnp.int32)
    offsets = (jnp.cumsum(counts) - counts).astype(jnp.int32)
    order_pad = jnp.concatenate([order, jnp.zeros((capacity,), jnp.int32)])
    start_out = jnp.zeros((TOKENS, D), jnp.float32)

    def one_expert(total_out, expert):
        slot_ids = lax.dynamic_slice_in_dim(order_pad, offsets[expert], capacity).astype(jnp.int32)
        valid = jnp.arange(capacity, dtype=jnp.int32) < counts[expert]
        tok_ids = (slot_ids // TOP).astype(jnp.int32)
        weights = jnp.where(valid, flat_gates[slot_ids], jnp.zeros((), jnp.float32))
        w_gate = gate_weight[expert]
        w_up = up_weight[expert]
        coef_gate, coef_up = coefficients(tokens[tok_ids], tangents[tok_ids], w_gate, w_up, down_weight[expert], readout)
        summed = jnp.zeros((capacity, D), jnp.float32)
        for block in range(N_TENSOR):
            lower = block * block_width
            upper = lower + block_width
            piece = jnp.dot(coef_gate[:, lower:upper], w_gate[:, lower:upper].T, preferred_element_type=jnp.float32)
            piece = piece + jnp.dot(coef_up[:, lower:upper], w_up[:, lower:upper].T, preferred_element_type=jnp.float32)
            summed = summed + piece.astype(jnp.bfloat16).astype(jnp.float32)
        total_out = total_out.at[tok_ids].add(weights[:, None] * summed)
        return total_out, None

    result, _ = lax.scan(one_expert, start_out, jnp.arange(EXPERTS, dtype=jnp.int32))
    return result.astype(jnp.bfloat16)
```

```python
import jax
import jax.numpy as jnp
from jax import lax
from jax.sharding import PartitionSpec as P


def shards(tokens, tangents, routes, gates, gate_weight, up_weight, down_weight, readout):
    experts = lax.axis_size("expert")
    parts = lax.axis_size("tensor")
    tok_rows, top_count = routes.shape
    most = tok_rows * top_count * 5 // (4 * experts)
    share = most // parts
    mine = lax.axis_index("tensor")

    named = routes[:, :, None] == jnp.arange(experts, dtype=jnp.int32)[None, None, :]
    chosen = jnp.any(named, axis=1)
    gate_of = jnp.sum(jnp.where(named, gates[:, :, None], 0.0), axis=1)
    before = jnp.tril(jnp.ones((tok_rows, tok_rows), jnp.bfloat16), -1)
    position = jnp.dot(before, chosen.astype(jnp.bfloat16), preferred_element_type=jnp.float32)
    position = jnp.where(chosen, position.astype(jnp.int32), -1)
    places = jnp.arange(share, dtype=jnp.int32) * parts + mine
    here = position[:, :, None] == places[None, None, :]
    select = here.reshape(tok_rows, experts * share)
    weight = jnp.where(here, gate_of[:, :, None], 0.0).reshape(tok_rows, experts * share)

    w_gate = lax.all_gather(gate_weight[0], "tensor", axis=0)
    w_up = lax.all_gather(up_weight[0], "tensor", axis=0)
    back = jnp.dot(down_weight[0], readout, preferred_element_type=jnp.float32)
    back = lax.all_gather(back, "tensor", axis=0)

    wide = lax.all_gather(jnp.stack([tokens, tangents], 0), "tensor", axis=2, tiled=True)
    width = wide.shape[2]
    pick = select.astype(jnp.bfloat16)
    rows_of = (((0,), (0,)), ((), ()))
    send = jnp.concatenate(
        [lax.dot_general(pick, wide[i], rows_of, preferred_element_type=jnp.float32) for i in (0, 1)], 1
    ).astype(jnp.bfloat16)
    got = lax.all_to_all(send, "expert", split_axis=0, concat_axis=0, tiled=True)
    rows_x, rows_v = got[:, :width], got[:, width:]

    total = jnp.zeros((experts * share, width), jnp.float32)
    contract = (((1,), (1,)), ((), ()))
    for b in range(parts):
        h = jnp.dot(rows_x, w_gate[b], preferred_element_type=jnp.float32)
        u = jnp.dot(rows_x, w_up[b], preferred_element_type=jnp.float32)
        dh = jnp.dot(rows_v, w_gate[b], preferred_element_type=jnp.float32)
        du = jnp.dot(rows_v, w_up[b], preferred_element_type=jnp.float32)
        sig = jax.nn.sigmoid(h)
        first = sig * (1.0 + h * (1.0 - sig))
        second = sig * (1.0 - sig) * (2.0 + h * (1.0 - 2.0 * sig))
        coef_gate = (back[b][None, :] * (du * first + u * second * dh)).astype(jnp.bfloat16)
        coef_up = (back[b][None, :] * first * dh).astype(jnp.bfloat16)
        total = total + lax.dot_general(coef_gate, w_gate[b], contract, preferred_element_type=jnp.float32)
        total = total + lax.dot_general(coef_up, w_up[b], contract, preferred_element_type=jnp.float32)
    returned = lax.all_to_all(total.astype(jnp.bfloat16), "expert", split_axis=0, concat_axis=0, tiled=True)
    high = weight.astype(jnp.bfloat16)
    low = (weight - high.astype(jnp.float32)).astype(jnp.bfloat16)
    per_token = jnp.dot(high, returned, preferred_element_type=jnp.float32) + jnp.dot(
        low, returned, preferred_element_type=jnp.float32
    )
    result = lax.psum_scatter(per_token, "tensor", scatter_dimension=1, tiled=True)
    return result.astype(jnp.bfloat16)


def solution(mesh):
    return jax.shard_map(
        shards,
        mesh=mesh,
        in_specs=(
            P("expert", "tensor"),
            P("expert", "tensor"),
            P("expert", None),
            P("expert", None),
            P("expert", None, "tensor"),
            P("expert", None, "tensor"),
            P("expert", "tensor", None),
            P(),
        ),
        out_specs=P("expert", "tensor"),
        check_vma=False,
    )
```

```python
import functools

import jax
import jax.numpy as jnp
import numpy as np
from jax import lax
from jax.experimental import pallas as pl
from jax.experimental.pallas import tpu as pltpu
from jax.sharding import PartitionSpec as P

MESH = pl.DeviceIdType.MESH
NEAR = 8
F32 = jnp.float32
BF16 = jnp.bfloat16
NT = (((1,), (1,)), ((), ()))


def tables(nz, nd, share, parts):
    rows = nz * nd * 2 * share
    experts = nz * nd
    expand = np.zeros((rows, experts), np.float32)
    target = np.full((rows, 2), -100.0, np.float32)
    perm_out = np.zeros((rows, rows), np.float32)
    perm_back = np.zeros((rows, rows), np.float32)
    expand_back = np.zeros((experts, rows), np.float32)
    target_back = np.full((8, rows), -100.0, np.float32)
    for z in range(nz):
        for d in range(nd):
            for k in range(2):
                for q in range(share):
                    a = ((d * nz + z) * 2 + k) * share + q
                    b = ((z * 2 + k) * nd + d) * share + q
                    c = ((d * 2 + k) * nz + z) * share + q
                    e = z * nd + d
                    expand[a, e] = 1
                    target[a, k] = parts * q
                    perm_out[b, a] = 1
                    perm_back[c, b] = 1
                    expand_back[e, c] = 1
                    target_back[k, c] = parts * q
    return expand, target, perm_out, perm_back, expand_back, target_back


def kernel(
    dims,
    tok_ref, tan_ref, gw_ref, uw_ref, dw_ref,
    routes_ref, routes_t_ref, gates_ref, readout_ref,
    expand_ref, target_ref, perm_out_ref, perm_back_ref, expand_back_ref, target_back_ref,
    out_ref,
    T, S1, R1, S2, R2, W, H, C, acc, Q1, Q2, DW, BK, PTF, PTB, RS, P1, CB,
    local_sem, t_send, t_recv, w_send, w_recv, b_send, b_recv,
    s1_send, s1_recv, s2_send, s2_recv, q1_send, q1_recv, q2_send, q2_recv, r_send, r_recv,
):
    nz, nd, share, parts = dims
    toks, qw = tok_ref.shape
    depth, ff = gw_ref.shape[1:]
    half_depth = depth // 2
    experts = nz * nd
    m1, m2 = nz * 2 * share, nd * 2 * share
    group = nd * share
    me, y = lax.axis_index("expert"), lax.axis_index("tensor")
    z, d = me // nd, lax.rem(me, nd)
    up_y, down_y, far_y = lax.rem(y + 1, parts), lax.rem(y + parts - 1, parts), lax.rem(y + 2, parts)

    def near(dd):
        return (z * nd + dd, y)

    def along(zz):
        return (zz * nd + d, y)

    def across(yy):
        return (me, yy)

    def rows_at(i, n):
        return pl.ds(pl.multiple_of(i * n, n), n)

    def remote(src, dst, ss, rs, dev):
        return pltpu.make_async_remote_copy(
            src_ref=src, dst_ref=dst, send_sem=ss, recv_sem=rs, device_id=dev, device_id_type=MESH
        )

    barrier = pltpu.get_barrier_semaphore()
    for yy in (up_y, down_y, far_y):
        pl.semaphore_signal(barrier, inc=1, device_id=across(yy), device_id_type=MESH)

    @pl.loop(1, nd)
    def _(k):
        pl.semaphore_signal(barrier, inc=1, device_id=near(lax.rem(d + k, nd)), device_id_type=MESH)

    @pl.loop(1, nz)
    def _(k):
        pl.semaphore_signal(barrier, inc=1, device_id=along(lax.rem(z + k, nz)), device_id_type=MESH)

    local = [
        pltpu.make_async_copy(tok_ref, T.at[0, pl.ds(0, toks)], local_sem.at[0]),
        pltpu.make_async_copy(tan_ref, T.at[0, pl.ds(toks, toks)], local_sem.at[1]),
        pltpu.make_async_copy(dw_ref.at[0], DW, local_sem.at[2]),
        pltpu.make_async_copy(gw_ref.at[0], W.at[0, :, pl.ds(0, ff)], local_sem.at[3]),
        pltpu.make_async_copy(uw_ref.at[0], W.at[0, :, pl.ds(ff, ff)], local_sem.at[4]),
    ]
    for c in local:
        c.start()
    pl.semaphore_wait(barrier, 3 + nd - 1 + nz - 1)

    def t_own(slot, kind, to):
        return remote(
            (tok_ref, tan_ref)[kind], T.at[slot, pl.ds(kind * toks, toks)],
            t_send.at[slot, kind], t_recv.at[slot, kind], across(to),
        )

    def t_on(kind):
        part = pl.ds(kind * toks, toks)
        return remote(
            T.at[1 + kind, part], T.at[3, part], t_send.at[3, kind], t_recv.at[3, kind],
            across((up_y, down_y)[kind]),
        )

    def w_own(slot, half, mat, to):
        part = pl.ds(half * half_depth, half_depth)
        return remote(
            (gw_ref, uw_ref)[mat].at[0, part], W.at[slot, part, pl.ds(mat * ff, ff)],
            w_send.at[slot, half, mat], w_recv.at[slot, half, mat], across(to),
        )

    def w_on(half, mat):
        part, cols = pl.ds(half * half_depth, half_depth), pl.ds(mat * ff, ff)
        return remote(
            W.at[1 + half, part, cols], W.at[3, part, cols],
            w_send.at[3, half, mat], w_recv.at[3, half, mat], across((up_y, down_y)[half]),
        )

    own_t = [t_own(1, 0, up_y), t_own(2, 1, down_y), t_own(1, 1, up_y), t_own(2, 0, down_y)]
    for c in own_t:
        c.start()

    tr = routes_t_ref.shape[0]
    ids = lax.broadcasted_iota(jnp.int32, (experts, toks), 0)
    chosen = jnp.zeros((experts, toks), F32)
    for k in range(tr):
        chosen = jnp.where(routes_t_ref[pl.ds(k, 1), :] == ids, 1.0, chosen)
    earlier = (
        lax.broadcasted_iota(jnp.int32, (toks, toks), 0) < lax.broadcasted_iota(jnp.int32, (toks, toks), 1)
    ).astype(F32).astype(BF16)
    place = jnp.dot(chosen.astype(BF16), earlier, preferred_element_type=F32)
    place = jnp.where(chosen > 0.5, place, -1.0)
    mine = y.astype(F32)
    place = jnp.dot(expand_ref[...], place.astype(BF16), preferred_element_type=F32) - mine
    for kind in range(2):
        hit = place == target_ref[:, pl.ds(kind, 1)]
        P1[:, pl.ds(kind * toks, toks)] = jnp.where(hit, 1.0, 0.0).astype(BF16)

    def owner(j):
        return (y, down_y, up_y, far_y)[j]

    def s1_copy(j, to, slot):
        return remote(
            S1.at[j, rows_at(to, m1)], R1.at[j, rows_at(slot, m1)],
            s1_send.at[j, to], s1_recv.at[j, slot], near(to),
        )

    def s2_copy(j, to, slot):
        cols = pl.ds(pl.multiple_of(owner(j) * qw, qw), qw)
        return remote(
            S2.at[j, rows_at(to, m2)], R2.at[rows_at(slot, m2), cols],
            s2_send.at[j, to], s2_recv.at[j, slot], along(to),
        )

    def pack(j):
        S1[j] = jnp.dot(P1[...], T[j], preferred_element_type=F32).astype(BF16)

        @pl.loop(1, nd)
        def _(k):
            s1_copy(j, lax.rem(d + k, nd), d).start()

        R1[j, rows_at(d, m1)] = S1[j, rows_at(d, m1)]

    def turn(j):
        @pl.loop(1, nd)
        def _(k):
            s = lax.rem(d + nd - k, nd)
            s1_copy(j, s, s).wait_recv()

        S2[j] = jnp.dot(perm_out_ref[...], R1[j], preferred_element_type=F32).astype(BF16)

        @pl.loop(1, nz)
        def _(k):
            s2_copy(j, lax.rem(z + k, nz), z).start()

        cols = pl.ds(pl.multiple_of(owner(j) * qw, qw), qw)
        R2[rows_at(z, m2), cols] = S2[j, rows_at(z, m2)]

    local[0].wait()
    local[1].wait()
    pack(0)
    for slot in (1, 2):
        for kind in range(2):
            t_own(slot, kind, up_y).wait_recv()
    t_on(0).start()
    t_on(1).start()
    for i in range(2):
        for mat in range(2):
            w_own(1, i, mat, up_y).start()
            w_own(2, 1 - i, mat, down_y).start()
    pack(1)
    turn(0)
    pack(2)
    turn(1)
    for kind in range(2):
        t_on(kind).wait_recv()
    pack(3)
    turn(2)

    local[2].wait()
    vec = jnp.broadcast_to(readout_ref[...], (16, depth))
    BK[0] = lax.dot_general(vec, DW[...], NT, preferred_element_type=F32)[0:8]

    def b_copy(slot, to):
        return remote(BK.at[0], BK.at[slot], b_send.at[slot], b_recv.at[slot], across(to))

    for slot, to in ((1, up_y), (2, down_y), (3, far_y)):
        b_copy(slot, to).start()

    for mat in range(2):
        for half in range(2):
            w_own(1 + half, half, mat, up_y).wait_recv()
            w_on(half, mat).start()
    turn(3)

    idl = lax.broadcasted_iota(jnp.int32, (toks, experts), 1)
    named = jnp.zeros((toks, experts), F32)
    gate = jnp.zeros((toks, experts), F32)
    for k in range(tr):
        hit = routes_ref[:, pl.ds(k, 1)] == idl
        named = jnp.where(hit, 1.0, named)
        gate = jnp.where(hit, gates_ref[:, pl.ds(k, 1)], gate)
    before = (
        lax.broadcasted_iota(jnp.int32, (toks, toks), 1) < lax.broadcasted_iota(jnp.int32, (toks, toks), 0)
    ).astype(F32).astype(BF16)
    place = jnp.dot(before, named.astype(BF16), preferred_element_type=F32)
    place = jnp.where(named > 0.5, place, -1.0)
    spread = expand_back_ref[...]
    place = jnp.dot(place.astype(BF16), spread, preferred_element_type=F32) - mine
    high = gate.astype(BF16)
    low = (gate - high.astype(F32)).astype(BF16)
    high = jnp.dot(high, spread, preferred_element_type=F32)
    low = jnp.dot(low, spread, preferred_element_type=F32)
    for half in range(2):
        hit = place == target_back_ref[pl.ds(half, 1), :]
        CB[pl.ds(2 * half * toks, toks)] = jnp.where(hit, high, 0.0).astype(BF16)
        CB[pl.ds((2 * half + 1) * toks, toks)] = jnp.where(hit, low, 0.0).astype(BF16)

    for j in range(4):
        @pl.loop(1, nz)
        def _(k):
            s = lax.rem(z + nz - k, nz)
            s2_copy(j, s, s).wait_recv()

    def block(slot):
        H[...] = jnp.dot(R2[...], W[slot], preferred_element_type=F32)
        back = BK[slot, 0:1]

        @pl.loop(0, nz // 2)
        def _(i):
            at = rows_at(i, 4 * group)
            gate_side, up_side = H[at, 0:ff], H[at, ff:]
            gate_out, up_out = [], []
            for s in range(2):
                lo = 2 * s * group
                h, dh = gate_side[lo : lo + group], gate_side[lo + group : lo + 2 * group]
                u, du = up_side[lo : lo + group], up_side[lo + group : lo + 2 * group]
                sig = jax.nn.sigmoid(h)
                first = sig * (1.0 + h * (1.0 - sig))
                second = sig * (1.0 - sig) * (2.0 + h * (1.0 - 2.0 * sig))
                gate_out.append(back * (du * first + u * second * dh))
                up_out.append(back * first * dh)
            to = rows_at(i, 2 * group)
            C[to, 0:ff] = jnp.concatenate(gate_out, 0).astype(BF16)
            C[to, ff:] = jnp.concatenate(up_out, 0).astype(BF16)

    def product(slot, n):
        part = pl.ds(pl.multiple_of(n * qw, qw), qw)
        return lax.dot_general(C[...], W[slot, part], NT, preferred_element_type=F32)

    local[3].wait()
    local[4].wait()
    block(0)
    for n in range(4):
        acc[n] = product(0, n)
    for slot in (1, 2):
        b_copy(slot, up_y).wait_recv()
        for half in range(2):
            if half != slot - 1:
                for mat in range(2):
                    w_own(slot, half, mat, up_y).wait_recv()
        block(slot)
        for n in range(4):
            acc[n] += product(slot, n)
    b_copy(3, up_y).wait_recv()
    for half in range(2):
        for mat in range(2):
            w_on(half, mat).wait_recv()
    block(3)

    for j in range(4):
        @pl.loop(1, nd)
        def _(k):
            s1_copy(j, lax.rem(d + k, nd), d).wait_send()

    def q1_copy(c, to, slot):
        return remote(
            S1.at[c, rows_at(to, m2)], Q1.at[c, rows_at(slot, m2)],
            q1_send.at[c, to], q1_recv.at[c, slot], along(to),
        )

    def q2_copy(c, to, slot):
        return remote(
            S1.at[2 + c, rows_at(to, m1)], Q2.at[c, rows_at(slot, m1)],
            q2_send.at[c, to], q2_recv.at[c, slot], near(to),
        )

    for c in range(2):
        for half in range(2):
            acc[2 * half + c] += product(3, 2 * half + c)

        @pl.loop(0, nz)
        def _(i):
            at = rows_at(i, group)
            both = jnp.concatenate([acc[c, at], acc[2 + c, at]], 0)
            S1[c, rows_at(i, m2)] = both.astype(BF16)

        @pl.loop(1, nz)
        def _(k):
            q1_copy(c, lax.rem(z + k, nz), z).start()

        Q1[c, rows_at(z, m2)] = S1[c, rows_at(z, m2)]

    for c in range(2):
        @pl.loop(1, nz)
        def _(k):
            s = lax.rem(z + nz - k, nz)
            q1_copy(c, s, s).wait_recv()

        S1[2 + c] = jnp.dot(perm_back_ref[...], Q1[c], preferred_element_type=F32).astype(BF16)

        @pl.loop(1, nd)
        def _(k):
            q2_copy(c, lax.rem(d + k, nd), d).start()

        Q2[c, rows_at(d, m1)] = S1[2 + c, rows_at(d, m1)]

    for c in range(2):
        @pl.loop(1, nd)
        def _(k):
            s = lax.rem(d + nd - k, nd)
            q2_copy(c, s, s).wait_recv()

        summed = jnp.dot(CB[...], Q2[c], preferred_element_type=F32)
        for half in range(2):
            lo = 2 * half * toks
            full = summed[lo : lo + toks] + summed[lo + toks : lo + 2 * toks]
            PTF[2 * half + c] = full
            PTB[2 * half + c] = full.astype(BF16)

    def r_copy(slot, to):
        return remote(PTB.at[to], RS.at[slot], r_send.at[slot], r_recv.at[slot], across(to))

    for slot, to in ((0, up_y), (1, down_y), (2, far_y)):
        r_copy(slot, to).start()
    total = PTF[y]
    for slot, to in ((0, up_y), (1, down_y), (2, far_y)):
        r_copy(slot, to).wait_recv()
        total = total + RS[slot].astype(F32)
    out_ref[...] = total.astype(BF16)

    for slot, to in ((0, up_y), (1, down_y), (2, far_y)):
        r_copy(slot, to).wait_send()
        b_copy(slot + 1, to).wait_send()
    for c in own_t:
        c.wait_send()
    for a in range(2):
        t_on(a).wait_send()
        for mat in range(2):
            w_own(1, a, mat, up_y).wait_send()
            w_own(2, a, mat, down_y).wait_send()
            w_on(a, mat).wait_send()
    for j in range(4):
        @pl.loop(1, nz)
        def _(k):
            s2_copy(j, lax.rem(z + k, nz), z).wait_send()
    for c in range(2):
        @pl.loop(1, nz)
        def _(k):
            q1_copy(c, lax.rem(z + k, nz), z).wait_send()

        @pl.loop(1, nd)
        def _(k):
            q2_copy(c, lax.rem(d + k, nd), d).wait_send()


def shards(near, tokens, tangents, routes, gates, gate_weight, up_weight, down_weight, readout):
    experts, parts = lax.axis_size("expert"), lax.axis_size("tensor")
    toks, qw = tokens.shape
    depth, ff = gate_weight.shape[1:]
    most = toks * routes.shape[1] * 5 // (4 * experts)
    share = most // parts
    nd, nz = near, experts // near
    rows = experts * share * 2
    expand, target, perm_out, perm_back, expand_back, target_back = tables(nz, nd, share, parts)
    hbm, vmem = pl.BlockSpec(memory_space=pl.ANY), pl.BlockSpec(memory_space=pltpu.VMEM)
    dma = pltpu.SemaphoreType.DMA
    return pl.pallas_call(
        functools.partial(kernel, (nz, nd, share, parts)),
        out_shape=jax.ShapeDtypeStruct((toks, qw), BF16),
        in_specs=[hbm] * 5 + [vmem] * 10,
        out_specs=vmem,
        scratch_shapes=[
            pltpu.VMEM((4, 2 * toks, qw), BF16),
            pltpu.VMEM((4, rows, qw), BF16),
            pltpu.VMEM((4, rows, qw), BF16),
            pltpu.VMEM((4, rows, qw), BF16),
            pltpu.VMEM((rows, depth), BF16),
            pltpu.VMEM((4, depth, 2 * ff), BF16),
            pltpu.VMEM((rows, 2 * ff), F32),
            pltpu.VMEM((rows // 2, 2 * ff), BF16),
            pltpu.VMEM((4, rows // 2, qw), F32),
            pltpu.VMEM((2, rows, qw), BF16),
            pltpu.VMEM((2, rows, qw), BF16),
            pltpu.VMEM((ff, depth), BF16),
            pltpu.VMEM((4, 8, ff), F32),
            pltpu.VMEM((4, toks, qw), F32),
            pltpu.VMEM((4, toks, qw), BF16),
            pltpu.VMEM((3, toks, qw), BF16),
            pltpu.VMEM((rows, 2 * toks), BF16),
            pltpu.VMEM((4 * toks, rows), BF16),
            dma((5,)),
            dma((4, 2)), dma((4, 2)),
            dma((4, 2, 2)), dma((4, 2, 2)),
            dma((4,)), dma((4,)),
            dma((4, nd)), dma((4, nd)),
            dma((4, nz)), dma((4, nz)),
            dma((2, nz)), dma((2, nz)),
            dma((2, nd)), dma((2, nd)),
            dma((3,)), dma((3,)),
        ],
        compiler_params=pltpu.CompilerParams(
            collective_id=0, has_side_effects=True, vmem_limit_bytes=62 * 2**20
        ),
    )(
        tokens, tangents, gate_weight, up_weight, down_weight,
        routes, routes.T, gates, readout.reshape(1, depth),
        jnp.asarray(expand, BF16), jnp.asarray(target, F32), jnp.asarray(perm_out, BF16),
        jnp.asarray(perm_back, BF16), jnp.asarray(expand_back, BF16), jnp.asarray(target_back, F32),
    )


def solution(mesh):
    return jax.shard_map(
        functools.partial(shards, NEAR),
        mesh=mesh,
        in_specs=(
            P("expert", "tensor"),
            P("expert", "tensor"),
            P("expert", None),
            P("expert", None),
            P("expert", None, "tensor"),
            P("expert", None, "tensor"),
            P("expert", "tensor", None),
            P(),
        ),
        out_specs=P("expert", "tensor"),
        check_vma=False,
    )
```

```python
import functools

import jax
import jax.numpy as jnp
import numpy as np
from jax import lax
from jax.experimental import pallas as pl
from jax.experimental.pallas import tpu as pltpu
from jax.sharding import PartitionSpec as P

MESH = pl.DeviceIdType.MESH
NEAR = 8
F32 = jnp.float32
BF16 = jnp.bfloat16
NT = (((1,), (1,)), ((), ()))


def tables(nz, nd, share, parts):
    rows = nz * nd * 2 * share
    experts = nz * nd
    expand = np.zeros((2, rows, experts), np.float32)
    target = np.full((rows, 2), -100.0, np.float32)
    to_z = np.zeros((rows, rows), np.float32)
    expand_back = np.zeros((2, experts, rows), np.float32)
    target_back = np.full((8, rows), -100.0, np.float32)
    for z in range(nz):
        for d in range(nd):
            for k in range(2):
                for q in range(share):
                    by_z = ((z * 2 + k) * nd + d) * share + q
                    by_d = ((d * 2 + k) * nz + z) * share + q
                    for own in range(2):
                        e = z * nd + d // 2 * 2 + own
                        expand[own, by_z, e] = 1
                        expand_back[own, e, by_d] = 1
                    target[by_z, k] = parts * q + d % 2
                    target_back[k, by_d] = parts * q + d % 2
                    to_z[by_z, by_d] = 1
    return expand, target, to_z, to_z.T, expand_back, target_back


def kernel(
    dims,
    tok_ref, tan_ref, gw_ref, uw_ref, dw_ref,
    routes_ref, routes_t_ref, gates_ref, readout_ref,
    expand_ref, target_ref, to_z_ref, to_d_ref, expand_back_ref, target_back_ref,
    out_ref,
    T, S1, R1, S2, R2, W, H, C, A, Q1, Q2, DW, BO, BK, PTF, PTB, RS, X0, PZ, PD, CB,
    local_sem, t_send, t_recv, w_send, w_recv, b_send, b_recv,
    s1_send, s1_recv, s2_send, s2_recv, q1_send, q1_recv, q2_send, q2_recv, r_send, r_recv,
):
    nz, nd, share, parts = dims
    toks, qw = tok_ref.shape
    depth, ff = gw_ref.shape[1:]
    half_depth = depth // 2
    experts = nz * nd
    m1, m2 = nz * 2 * share, nd * 2 * share
    group = nd * share
    me, y = lax.axis_index("expert"), lax.axis_index("tensor")
    z, d = me // nd, lax.rem(me, nd)
    own, odd, core = y // 2, lax.rem(y, 2), lax.rem(me, 2)
    home = core == own
    away = core != own
    mate, outer, far = y + 1 - 2 * odd, parts - 1 - y, lax.rem(y + 2, parts)
    others = (mate, outer, far)

    def near(dd):
        return (z * nd + dd, y)

    def along(zz):
        return (zz * nd + d, y)

    def across(yy, cc=None):
        return (me if cc is None else me - core + cc, yy)

    def rows_at(i, n):
        return pl.ds(pl.multiple_of(i * n, n), n)

    def remote(src, dst, ss, rs, dev):
        return pltpu.make_async_remote_copy(
            src_ref=src, dst_ref=dst, send_sem=ss, recv_sem=rs, device_id=dev, device_id_type=MESH
        )

    barrier = pltpu.get_barrier_semaphore()
    for yy in others:
        for cc in range(2):
            pl.semaphore_signal(barrier, inc=1, device_id=across(yy, cc), device_id_type=MESH)

    @pl.loop(1, nd)
    def _(k):
        pl.semaphore_signal(barrier, inc=1, device_id=near(lax.rem(d + k, nd)), device_id_type=MESH)

    @pl.loop(1, nz)
    def _(k):
        pl.semaphore_signal(barrier, inc=1, device_id=along(lax.rem(z + k, nz)), device_id_type=MESH)

    local = [
        pltpu.make_async_copy(tok_ref, T.at[0, pl.ds(0, toks)], local_sem.at[0]),
        pltpu.make_async_copy(tan_ref, T.at[0, pl.ds(toks, toks)], local_sem.at[1]),
        pltpu.make_async_copy(dw_ref.at[0], DW, local_sem.at[2]),
    ]
    stage = [
        pltpu.make_async_copy(gw_ref.at[0], W.at[0, :, pl.ds(0, ff)], local_sem.at[3]),
        pltpu.make_async_copy(uw_ref.at[0], W.at[0, :, pl.ds(ff, ff)], local_sem.at[4]),
    ]
    for c in local:
        c.start()

    @pl.when(home)
    def _():
        for c in stage:
            c.start()

    pl.semaphore_wait(barrier, 2 * 3 + nd - 1 + nz - 1)

    def t_own(slot, kind):
        return remote(
            (tok_ref, tan_ref)[kind], T.at[slot, pl.ds(kind * toks, toks)],
            t_send.at[slot, kind], t_recv.at[slot, kind], across(others[slot - 1]),
        )

    def t_on():
        return remote(T.at[1], T.at[3], t_send.at[3, 0], t_recv.at[3, 0], across(outer))

    def w_from(slot, half, mat, yy, cc, sem):
        part = pl.ds(half * half_depth, half_depth)
        return remote(
            (gw_ref, uw_ref)[mat].at[0, part], W.at[slot, part, pl.ds(mat * ff, ff)],
            w_send.at[sem, half, mat], w_recv.at[slot, half, mat], across(yy, cc),
        )

    def w_on(slot, half, mat, slot_to, yy, cc, sem):
        part, cols = pl.ds(pl.multiple_of(half * half_depth, half_depth), half_depth), pl.ds(mat * ff, ff)
        return remote(
            W.at[slot, part, cols], W.at[slot_to, part, cols],
            w_send.at[sem, half, mat], w_recv.at[slot_to, half, mat], across(yy, cc),
        )

    pieces = [(half, mat) for mat in range(2) for half in range(2)]
    for slot in (1, 2):
        for kind in range(2):
            t_own(slot, kind).start()

    @pl.when(home)
    def _():
        for half, mat in pieces:
            w_from(1, half, mat, mate, half, 0).start()
        for half, mat in pieces:
            w_from(0, half, mat, y, 1 - core, 1).start()

    @pl.when(away)
    def _():
        for half, mat in pieces:
            w_from(2, half, mat, outer, half, 0).start()

    def w_get(slot, half, mat):
        w_on(slot, half, mat, slot, y, 1 - core, slot + 1).wait_recv()

    def pass_on(slot, mat):
        w_get(slot, core, mat)
        w_on(slot, core, mat, slot, y, 1 - core, slot + 1).start()
        if slot == 2:
            w_on(2, core, mat, 3, mate, core, 5).start()

    tr = routes_t_ref.shape[0]
    ids = lax.broadcasted_iota(jnp.int32, (experts, toks), 0)
    chosen = jnp.zeros((experts, toks), F32)
    for k in range(tr):
        chosen = jnp.where(routes_t_ref[pl.ds(k, 1), :] == ids, 1.0, chosen)
    earlier = (
        lax.broadcasted_iota(jnp.int32, (toks, toks), 0) < lax.broadcasted_iota(jnp.int32, (toks, toks), 1)
    ).astype(F32).astype(BF16)
    place = jnp.dot(chosen.astype(BF16), earlier, preferred_element_type=F32)
    place = jnp.where(chosen > 0.5, place, -1.0)
    mine = (2 * odd).astype(F32)
    place = jnp.dot(expand_ref[own], place.astype(BF16), preferred_element_type=F32) - mine
    for kind in range(2):
        hit = place == target_ref[:, pl.ds(kind, 1)]
        PZ[:, pl.ds(kind * toks, toks)] = jnp.where(hit, 1.0, 0.0).astype(BF16)

    def owner(j):
        return (y, mate, outer, far)[j]

    def cols_of(j):
        return pl.ds(pl.multiple_of(owner(j) * qw, qw), qw)

    def s1_copy(j, to, slot):
        at = rows_at(slot, m1)
        return remote(
            S1.at[j, rows_at(to, m1)], R1.at[j, at] if j else X0.at[at],
            s1_send.at[j, to], s1_recv.at[j, slot], near(to),
        )

    def s2_copy(j, to, slot):
        at = rows_at(slot, m2)
        return remote(
            S2.at[j, rows_at(to, m2)], R2.at[at, cols_of(j)] if j else R1.at[0, at],
            s2_send.at[j, to], s2_recv.at[j, slot], along(to),
        )

    def send_near(copy, j):
        @pl.loop(1, nd)
        def _(k):
            copy(j, lax.rem(d + k, nd), d).start()

    def send_along(copy, j):
        @pl.loop(1, nz)
        def _(k):
            copy(j, lax.rem(z + k, nz), z).start()

    def get_near(copy, j):
        @pl.loop(1, nd)
        def _(k):
            s = lax.rem(d + nd - k, nd)
            copy(j, s, s).wait_recv()

    def get_along(copy, j):
        @pl.loop(1, nz)
        def _(k):
            s = lax.rem(z + nz - k, nz)
            copy(j, s, s).wait_recv()

    def sent_near(copy, j):
        @pl.loop(1, nd)
        def _(k):
            copy(j, lax.rem(d + k, nd), d).wait_send()

    def sent_along(copy, j):
        @pl.loop(1, nz)
        def _(k):
            copy(j, lax.rem(z + k, nz), z).wait_send()

    def mix(table, rows):
        return jnp.dot(table, rows, preferred_element_type=F32).astype(BF16)

    def pack(j):
        S1[j] = mix(PD[...], T[j])
        send_near(s1_copy, j)
        R1[j, rows_at(d, m1)] = S1[j, rows_at(d, m1)]

    def turn(j):
        get_near(s1_copy, j)
        S2[j] = mix(to_z_ref[...], R1[j])
        send_along(s2_copy, j)
        R2[rows_at(z, m2), cols_of(j)] = S2[j, rows_at(z, m2)]

    local[0].wait()
    local[1].wait()
    S2[0] = mix(PZ[...], T[0])
    send_along(s2_copy, 0)
    R1[0, rows_at(z, m2)] = S2[0, rows_at(z, m2)]
    PD[...] = mix(to_d_ref[...], PZ[...])

    local[2].wait()
    vec = jnp.broadcast_to(readout_ref[...], (16, depth))
    BO[...] = lax.dot_general(vec, DW[...], NT, preferred_element_type=F32)[0:8]

    def b_copy(slot, i, yy, cc):
        return remote(BO, BK.at[slot], b_send.at[i], b_recv.at[slot], across(yy, cc))

    def b_home():
        return [b_copy(0, 0, y, 1 - core), b_copy(1, 1, mate, 0), b_copy(1, 2, mate, 1)]

    def b_away():
        return [b_copy(slot, 2 * slot - 4 + cc, yy, cc) for slot, yy in ((2, outer), (3, far)) for cc in range(2)]

    @pl.when(home)
    def _():
        for c in b_home():
            c.start()
        BK[0] = BO[...]

    @pl.when(away)
    def _():
        for c in b_away():
            c.start()

    for kind in range(2):
        t_own(1, kind).wait_recv()
    t_on().start()
    pack(1)
    for kind in range(2):
        t_own(2, kind).wait_recv()
    turn(1)
    pack(2)
    pass_on(2, 0)
    t_on().wait_recv()
    pack(3)
    turn(2)
    pass_on(2, 1)
    pass_on(1, 0)
    get_along(s2_copy, 0)
    S1[0] = mix(to_d_ref[...], R1[0])
    send_near(s1_copy, 0)
    X0[rows_at(d, m1)] = S1[0, rows_at(d, m1)]
    turn(3)
    pass_on(1, 1)

    idl = lax.broadcasted_iota(jnp.int32, (toks, experts), 1)
    named = jnp.zeros((toks, experts), F32)
    gate = jnp.zeros((toks, experts), F32)
    for k in range(tr):
        hit = routes_ref[:, pl.ds(k, 1)] == idl
        named = jnp.where(hit, 1.0, named)
        gate = jnp.where(hit, gates_ref[:, pl.ds(k, 1)], gate)
    before = (
        lax.broadcasted_iota(jnp.int32, (toks, toks), 1) < lax.broadcasted_iota(jnp.int32, (toks, toks), 0)
    ).astype(F32).astype(BF16)
    place = jnp.dot(before, named.astype(BF16), preferred_element_type=F32)
    place = jnp.where(named > 0.5, place, -1.0)
    spread = expand_back_ref[own]
    place = jnp.dot(place.astype(BF16), spread, preferred_element_type=F32) - mine
    high = gate.astype(BF16)
    low = (gate - high.astype(F32)).astype(BF16)
    high = jnp.dot(high, spread, preferred_element_type=F32)
    low = jnp.dot(low, spread, preferred_element_type=F32)
    for half in range(2):
        hit = place == target_back_ref[pl.ds(half, 1), :]
        CB[0, pl.ds(2 * half * toks, toks)] = jnp.where(hit, high, 0.0).astype(BF16)
        CB[0, pl.ds((2 * half + 1) * toks, toks)] = jnp.where(hit, low, 0.0).astype(BF16)
    CB[1] = mix(CB[0], to_d_ref[...])

    get_near(s1_copy, 0)
    R2[:, cols_of(0)] = mix(to_z_ref[...], X0[...])

    pass_on(3, 0)
    pass_on(3, 1)

    @pl.when(home)
    def _():
        for c in stage:
            c.wait()

    @pl.when(away)
    def _():
        for half, mat in pieces:
            w_get(0, half, mat)
        b_copy(0, 0, y, 1 - core).wait_recv()

    for slot in (1, 2, 3):
        for mat in range(2):
            w_get(slot, 1 - core, mat)
        b_copy(slot, 0, y, 1 - core).wait_recv()

    for j in range(4):
        if j:
            get_along(s2_copy, j)
        cols = cols_of(j)
        for slot in range(4):
            H[slot] = (H[slot] if j else 0.0) + jnp.dot(R2[:, cols], W[slot, cols], preferred_element_type=F32)

    for slot in range(4):
        back = BK[slot, 0:1]

        @pl.loop(0, nz // 2)
        def _(i):
            at = rows_at(i, 4 * group)
            gate_side, up_side = H[slot, at, 0:ff], H[slot, at, ff:]
            gate_out, up_out = [], []
            for s in range(2):
                lo = 2 * s * group
                h, dh = gate_side[lo : lo + group], gate_side[lo + group : lo + 2 * group]
                u, du = up_side[lo : lo + group], up_side[lo + group : lo + 2 * group]
                sig = jax.nn.sigmoid(h)
                first = sig * (1.0 + h * (1.0 - sig))
                second = sig * (1.0 - sig) * (2.0 + h * (1.0 - 2.0 * sig))
                gate_out.append(back * (du * first + u * second * dh))
                up_out.append(back * first * dh)
            to = rows_at(i, 2 * group)
            C[slot, to, 0:ff] = jnp.concatenate(gate_out, 0).astype(BF16)
            C[slot, to, ff:] = jnp.concatenate(up_out, 0).astype(BF16)

    def product(n):
        total = 0.0
        for slot in range(4):
            total = total + lax.dot_general(
                C[slot], W[slot, pl.ds(n * qw, qw)], NT, preferred_element_type=F32
            )
        return total

    for j in range(4):
        sent_near(s1_copy, j)

    def q1_copy(c, to, slot):
        return remote(
            S1.at[c, rows_at(to, m2)], Q1.at[c, rows_at(slot, m2)],
            q1_send.at[c, to], q1_recv.at[c, slot], along(to),
        )

    def q2_copy(c, to, slot):
        return remote(
            S1.at[2 + c, rows_at(to, m1)], Q2.at[c, rows_at(slot, m1)],
            q2_send.at[c, to], q2_recv.at[c, slot], near(to),
        )

    def go_along(c):
        send_along(q1_copy, c)
        Q1[c, rows_at(z, m2)] = S1[c, rows_at(z, m2)]

    def go_near(c, rows):
        S1[2 + c] = mix(to_d_ref[...], rows)
        send_near(q2_copy, c)
        Q2[c, rows_at(d, m1)] = S1[2 + c, rows_at(d, m1)]

    def r_copy(slot, to):
        return remote(PTB.at[to], RS.at[slot], r_send.at[slot], r_recv.at[slot], across(to))

    def combine(c, rows):
        summed = jnp.dot(CB[c], rows, preferred_element_type=F32)
        for half in range(2):
            lo = 2 * half * toks
            full = summed[lo : lo + toks] + summed[lo + toks : lo + 2 * toks]
            PTF[2 * half + c] = full
            PTB[2 * half + c] = full.astype(BF16)
        for slot, to in enumerate(others):
            @pl.when(lax.rem(to, 2) == c)
            def _():
                r_copy(slot, to).start()

    for c in range(2):
        for half in range(2):
            A[half] = product(2 * half + c)

        @pl.loop(0, nz)
        def _(i):
            at = rows_at(i, group)
            both = jnp.concatenate([A[0, at], A[1, at]], 0)
            S1[c, rows_at(i, m2)] = both.astype(BF16)

        if c == 0:
            go_along(0)
        else:
            go_near(1, S1[1])
    get_near(q2_copy, 1)
    S1[1] = mix(to_z_ref[...], Q2[1])
    go_along(1)
    get_along(q1_copy, 0)
    go_near(0, Q1[0])
    get_near(q2_copy, 0)
    combine(0, Q2[0])
    get_along(q1_copy, 1)
    combine(1, Q1[1])

    total = PTF[y]
    for slot, to in enumerate(others):
        r_copy(slot, to).wait_recv()
        total = total + RS[slot].astype(F32)
    out_ref[...] = total.astype(BF16)

    for slot, to in enumerate(others):
        r_copy(slot, to).wait_send()
    for slot in (1, 2):
        for kind in range(2):
            t_own(slot, kind).wait_send()
    t_on().wait_send()

    @pl.when(home)
    def _():
        for half, mat in pieces:
            w_from(1, half, mat, mate, half, 0).wait_send()
            w_from(0, half, mat, y, 1 - core, 1).wait_send()
        for c in b_home():
            c.wait_send()

    @pl.when(away)
    def _():
        for half, mat in pieces:
            w_from(2, half, mat, outer, half, 0).wait_send()
        for c in b_away():
            c.wait_send()

    for mat in range(2):
        for slot in (1, 2, 3):
            w_on(slot, core, mat, slot, y, 1 - core, slot + 1).wait_send()
        w_on(2, core, mat, 3, mate, core, 5).wait_send()
    for j in range(4):
        sent_along(s2_copy, j)
    for c in range(2):
        sent_along(q1_copy, c)
        sent_near(q2_copy, c)


def shards(near, tokens, tangents, routes, gates, gate_weight, up_weight, down_weight, readout):
    experts, parts = lax.axis_size("expert"), lax.axis_size("tensor")
    toks, qw = tokens.shape
    depth, ff = gate_weight.shape[1:]
    most = toks * routes.shape[1] * 5 // (4 * experts)
    share = most // parts
    nd, nz = near, experts // near
    rows = experts * share * 2
    expand, target, to_z, to_d, expand_back, target_back = tables(nz, nd, share, parts)
    hbm, vmem = pl.BlockSpec(memory_space=pl.ANY), pl.BlockSpec(memory_space=pltpu.VMEM)
    dma = pltpu.SemaphoreType.DMA
    return pl.pallas_call(
        functools.partial(kernel, (nz, nd, share, parts)),
        out_shape=jax.ShapeDtypeStruct((toks, qw), BF16),
        in_specs=[hbm] * 5 + [vmem] * 10,
        out_specs=vmem,
        scratch_shapes=[
            pltpu.VMEM((4, 2 * toks, qw), BF16),
            pltpu.VMEM((4, rows, qw), BF16),
            pltpu.VMEM((4, rows, qw), BF16),
            pltpu.VMEM((4, rows, qw), BF16),
            pltpu.VMEM((rows, depth), BF16),
            pltpu.VMEM((4, depth, 2 * ff), BF16),
            pltpu.VMEM((4, rows, 2 * ff), F32),
            pltpu.VMEM((4, rows // 2, 2 * ff), BF16),
            pltpu.VMEM((2, rows // 2, qw), F32),
            pltpu.VMEM((2, rows, qw), BF16),
            pltpu.VMEM((2, rows, qw), BF16),
            pltpu.VMEM((ff, depth), BF16),
            pltpu.VMEM((8, ff), F32),
            pltpu.VMEM((4, 8, ff), F32),
            pltpu.VMEM((4, toks, qw), F32),
            pltpu.VMEM((4, toks, qw), BF16),
            pltpu.VMEM((3, toks, qw), BF16),
            pltpu.VMEM((rows, qw), BF16),
            pltpu.VMEM((rows, 2 * toks), BF16),
            pltpu.VMEM((rows, 2 * toks), BF16),
            pltpu.VMEM((2, 4 * toks, rows), BF16),
            dma((5,)),
            dma((4, 2)), dma((4, 2)),
            dma((6, 2, 2)), dma((4, 2, 2)),
            dma((4,)), dma((4,)),
            dma((4, nd)), dma((4, nd)),
            dma((4, nz)), dma((4, nz)),
            dma((2, nz)), dma((2, nz)),
            dma((2, nd)), dma((2, nd)),
            dma((3,)), dma((3,)),
        ],
        compiler_params=pltpu.CompilerParams(
            collective_id=0, has_side_effects=True, vmem_limit_bytes=62 * 2**20
        ),
    )(
        tokens, tangents, gate_weight, up_weight, down_weight,
        routes, routes.T, gates, readout.reshape(1, depth),
        jnp.asarray(expand, BF16), jnp.asarray(target, F32), jnp.asarray(to_z, BF16),
        jnp.asarray(to_d, BF16), jnp.asarray(expand_back, BF16), jnp.asarray(target_back, F32),
    )


def solution(mesh):
    return jax.shard_map(
        functools.partial(shards, NEAR),
        mesh=mesh,
        in_specs=(
            P("expert", "tensor"),
            P("expert", "tensor"),
            P("expert", None),
            P("expert", None),
            P("expert", None, "tensor"),
            P("expert", None, "tensor"),
            P("expert", "tensor", None),
            P(),
        ),
        out_specs=P("expert", "tensor"),
        check_vma=False,
    )
```

```python
import functools

import jax
import jax.numpy as jnp
import numpy as np
from jax import lax
from jax.experimental import pallas as pl
from jax.experimental.pallas import tpu as pltpu
from jax.sharding import PartitionSpec as P

MESH = pl.DeviceIdType.MESH
NEAR = 8
F32 = jnp.float32
BF16 = jnp.bfloat16
NT = (((1,), (1,)), ((), ()))


def tables(nz, nd, share, parts):
    rows = nz * nd * 2 * share
    experts = nz * nd
    expand = np.zeros((2, rows, experts), np.float32)
    target = np.full((rows, 2), -100.0, np.float32)
    to_z = np.zeros((rows, rows), np.float32)
    expand_back = np.zeros((2, experts, rows), np.float32)
    target_back = np.full((8, rows), -100.0, np.float32)
    for z in range(nz):
        for d in range(nd):
            for k in range(2):
                for q in range(share):
                    by_z = ((z * 2 + k) * nd + d) * share + q
                    by_d = ((d * 2 + k) * nz + z) * share + q
                    for own in range(2):
                        e = z * nd + d // 2 * 2 + own
                        expand[own, by_z, e] = 1
                        expand_back[own, e, by_d] = 1
                    target[by_z, k] = parts * q + d % 2
                    target_back[k, by_d] = parts * q + d % 2
                    to_z[by_z, by_d] = 1
    return expand, target, to_z, to_z.T, expand_back, target_back


def kernel(
    dims,
    tok_ref, tan_ref, gw_ref, uw_ref, dw_ref,
    routes_ref, gates_ref, readout_ref,
    expand_ref, target_ref, to_z_hbm, to_d_hbm, expand_back_ref, target_back_ref,
    out_ref,
    T, S1, R1, S2, R2, W, H, C, A, Q1, Q2, DW, BO, BK, PTF, PTB, RS, X0, PZ, PD, CB, to_z_ref, to_d_ref,
    local_sem, t_send, t_recv, w_send, w_recv, b_send, b_recv,
    s1_send, s1_recv, s2_send, s2_recv, q1_send, q1_recv, q2_send, q2_recv, r_send, r_recv,
):
    nz, nd, share, parts = dims
    toks, qw = tok_ref.shape
    depth, ff = gw_ref.shape[1:]
    half_depth = depth // 2
    experts = nz * nd
    m1, m2 = nz * 2 * share, nd * 2 * share
    group = nd * share
    me, y = lax.axis_index("expert"), lax.axis_index("tensor")
    z, d = me // nd, lax.rem(me, nd)
    own, odd, core = y // 2, lax.rem(y, 2), lax.rem(me, 2)
    home = core == own
    away = core != own
    mate, outer, far = y + 1 - 2 * odd, parts - 1 - y, lax.rem(y + 2, parts)
    others = (mate, outer, far)

    def near(dd):
        return (z * nd + dd, y)

    def along(zz):
        return (zz * nd + d, y)

    def across(yy, cc=None):
        return (me if cc is None else me - core + cc, yy)

    def rows_at(i, n):
        return pl.ds(pl.multiple_of(i * n, n), n)

    def remote(src, dst, ss, rs, dev):
        return pltpu.make_async_remote_copy(
            src_ref=src, dst_ref=dst, send_sem=ss, recv_sem=rs, device_id=dev, device_id_type=MESH
        )

    barrier = pltpu.get_barrier_semaphore()
    for yy in others:
        for cc in range(2):
            pl.semaphore_signal(barrier, inc=1, device_id=across(yy, cc), device_id_type=MESH)

    @pl.loop(1, nd)
    def _(k):
        pl.semaphore_signal(barrier, inc=1, device_id=near(lax.rem(d + k, nd)), device_id_type=MESH)

    @pl.loop(1, nz)
    def _(k):
        pl.semaphore_signal(barrier, inc=1, device_id=along(lax.rem(z + k, nz)), device_id_type=MESH)

    local = [
        pltpu.make_async_copy(tok_ref, T.at[0, pl.ds(0, toks)], local_sem.at[0]),
        pltpu.make_async_copy(tan_ref, T.at[0, pl.ds(toks, toks)], local_sem.at[1]),
        pltpu.make_async_copy(dw_ref.at[0], DW, local_sem.at[2]),
        pltpu.make_async_copy(to_d_hbm, to_d_ref, local_sem.at[5]),
        pltpu.make_async_copy(to_z_hbm, to_z_ref, local_sem.at[6]),
    ]
    stage = [
        pltpu.make_async_copy(gw_ref.at[0], W.at[0, :, pl.ds(0, ff)], local_sem.at[3]),
        pltpu.make_async_copy(uw_ref.at[0], W.at[0, :, pl.ds(ff, ff)], local_sem.at[4]),
    ]
    for c in local:
        c.start()

    @pl.when(home)
    def _():
        for c in stage:
            c.start()

    def t_own(slot, kind):
        return remote(
            (tok_ref, tan_ref)[kind], T.at[slot, pl.ds(kind * toks, toks)],
            t_send.at[slot, kind], t_recv.at[slot, kind], across(others[slot - 1]),
        )

    def t_on():
        return remote(T.at[1], T.at[3], t_send.at[3, 0], t_recv.at[3, 0], across(outer))

    def w_from(slot, half, mat, yy, cc, sem):
        part = pl.ds(half * half_depth, half_depth)
        return remote(
            (gw_ref, uw_ref)[mat].at[0, part], W.at[slot, part, pl.ds(mat * ff, ff)],
            w_send.at[sem, half, mat], w_recv.at[slot, half, mat], across(yy, cc),
        )

    def w_on(slot, half, mat, slot_to, yy, cc, sem):
        part, cols = pl.ds(pl.multiple_of(half * half_depth, half_depth), half_depth), pl.ds(mat * ff, ff)
        return remote(
            W.at[slot, part, cols], W.at[slot_to, part, cols],
            w_send.at[sem, half, mat], w_recv.at[slot_to, half, mat], across(yy, cc),
        )

    pieces = [(half, mat) for mat in range(2) for half in range(2)]

    def w_get(slot, half, mat):
        w_on(slot, half, mat, slot, y, 1 - core, slot + 1).wait_recv()

    def pass_on(slot, mat):
        w_get(slot, core, mat)
        w_on(slot, core, mat, slot, y, 1 - core, slot + 1).start()
        if slot == 2:
            w_on(2, core, mat, 3, mate, core, 5).start()

    top = routes_ref.shape[0]
    ids = lax.broadcasted_iota(jnp.int32, (experts, toks), 0)
    chosen = jnp.zeros((experts, toks), F32)
    for k in range(top):
        chosen = jnp.where(routes_ref[pl.ds(k, 1), :] == ids, 1.0, chosen)
    earlier = (
        lax.broadcasted_iota(jnp.int32, (toks, toks), 0) < lax.broadcasted_iota(jnp.int32, (toks, toks), 1)
    ).astype(F32).astype(BF16)
    place = jnp.dot(chosen.astype(BF16), earlier, preferred_element_type=F32)
    taken = jnp.where(chosen > 0.5, place, -1.0).astype(BF16)
    mine = (2 * odd).astype(F32)
    place = jnp.dot(expand_ref[own], taken, preferred_element_type=F32) - mine
    for kind in range(2):
        hit = place == target_ref[:, pl.ds(kind, 1)]
        PZ[:, pl.ds(kind * toks, toks)] = jnp.where(hit, 1.0, 0.0).astype(BF16)

    def owner(j):
        return (y, mate, outer, far)[j]

    def cols_of(j):
        return pl.ds(pl.multiple_of(owner(j) * qw, qw), qw)

    def s1_copy(j, to, slot):
        at = rows_at(slot, m1)
        return remote(
            S1.at[j, rows_at(to, m1)], R1.at[j, at] if j else X0.at[at],
            s1_send.at[j, to], s1_recv.at[j, slot], near(to),
        )

    def s2_copy(j, to, slot):
        at = rows_at(slot, m2)
        return remote(
            S2.at[j, rows_at(to, m2)], R2.at[at, cols_of(j)] if j else R1.at[0, at],
            s2_send.at[j, to], s2_recv.at[j, slot], along(to),
        )

    def send_near(copy, j):
        @pl.loop(1, nd)
        def _(k):
            copy(j, lax.rem(d + k, nd), d).start()

    def send_along(copy, j):
        @pl.loop(1, nz)
        def _(k):
            copy(j, lax.rem(z + k, nz), z).start()

    def get_near(copy, j):
        @pl.loop(1, nd)
        def _(k):
            s = lax.rem(d + nd - k, nd)
            copy(j, s, s).wait_recv()

    def get_along(copy, j):
        @pl.loop(1, nz)
        def _(k):
            s = lax.rem(z + nz - k, nz)
            copy(j, s, s).wait_recv()

    def sent_near(copy, j):
        @pl.loop(1, nd)
        def _(k):
            copy(j, lax.rem(d + k, nd), d).wait_send()

    def sent_along(copy, j):
        @pl.loop(1, nz)
        def _(k):
            copy(j, lax.rem(z + k, nz), z).wait_send()

    def mix(table, rows):
        return jnp.dot(table, rows, preferred_element_type=F32).astype(BF16)

    def pack(j):
        S1[j] = mix(PD[...], T[j])
        send_near(s1_copy, j)
        R1[j, rows_at(d, m1)] = S1[j, rows_at(d, m1)]

    def turn(j):
        get_near(s1_copy, j)
        S2[j] = mix(to_z_ref[...], R1[j])
        send_along(s2_copy, j)
        R2[rows_at(z, m2), cols_of(j)] = S2[j, rows_at(z, m2)]

    local[0].wait()
    local[1].wait()
    S2[0] = mix(PZ[...], T[0])
    pl.semaphore_wait(barrier, 2 * 3 + nd - 1 + nz - 1)
    send_along(s2_copy, 0)
    for slot in (1, 2):
        for kind in range(2):
            t_own(slot, kind).start()

    @pl.when(home)
    def _():
        for half, mat in pieces:
            w_from(1, half, mat, mate, half, 0).start()
        for half, mat in pieces:
            w_from(0, half, mat, y, 1 - core, 1).start()

    @pl.when(away)
    def _():
        for half, mat in pieces:
            w_from(2, half, mat, outer, half, 0).start()

    R1[0, rows_at(z, m2)] = S2[0, rows_at(z, m2)]
    local[3].wait()
    local[4].wait()
    PD[...] = mix(to_d_ref[...], PZ[...])

    local[2].wait()
    vec = jnp.broadcast_to(readout_ref[...][None, :], (16, depth))
    BO[...] = lax.dot_general(vec, DW[...], NT, preferred_element_type=F32)[0:8]

    def b_copy(slot, i, yy, cc):
        return remote(BO, BK.at[slot], b_send.at[i], b_recv.at[slot], across(yy, cc))

    def b_home():
        return [b_copy(0, 0, y, 1 - core), b_copy(1, 1, mate, 0), b_copy(1, 2, mate, 1)]

    def b_away():
        return [b_copy(slot, 2 * slot - 4 + cc, yy, cc) for slot, yy in ((2, outer), (3, far)) for cc in range(2)]

    @pl.when(home)
    def _():
        for c in b_home():
            c.start()
        BK[0] = BO[...]

    @pl.when(away)
    def _():
        for c in b_away():
            c.start()

    for kind in range(2):
        t_own(1, kind).wait_recv()
    t_on().start()
    pack(1)
    for kind in range(2):
        t_own(2, kind).wait_recv()
    turn(1)
    pack(2)
    pass_on(2, 0)
    t_on().wait_recv()
    pack(3)
    turn(2)
    pass_on(2, 1)
    pass_on(1, 0)
    get_along(s2_copy, 0)
    S1[0] = mix(to_d_ref[...], R1[0])
    send_near(s1_copy, 0)
    X0[rows_at(d, m1)] = S1[0, rows_at(d, m1)]
    turn(3)
    pass_on(1, 1)

    gate = jnp.zeros((experts, toks), F32)
    for k in range(top):
        gate = jnp.where(routes_ref[pl.ds(k, 1), :] == ids, gates_ref[pl.ds(k, 1), :], gate)
    high = gate.astype(BF16)
    low = (gate - high.astype(F32)).astype(BF16)
    place, high, low = [
        lax.dot_general(a, expand_back_ref[own], (((0,), (0,)), ((), ())), preferred_element_type=F32)
        for a in (taken, high, low)
    ]
    place = place - mine
    for half in range(2):
        hit = place == target_back_ref[pl.ds(half, 1), :]
        CB[0, pl.ds(2 * half * toks, toks)] = jnp.where(hit, high, 0.0).astype(BF16)
        CB[0, pl.ds((2 * half + 1) * toks, toks)] = jnp.where(hit, low, 0.0).astype(BF16)
    CB[1] = mix(CB[0], to_d_ref[...])

    get_near(s1_copy, 0)
    R2[:, cols_of(0)] = mix(to_z_ref[...], X0[...])

    pass_on(3, 0)
    pass_on(3, 1)

    @pl.when(home)
    def _():
        for c in stage:
            c.wait()

    @pl.when(away)
    def _():
        for half, mat in pieces:
            w_get(0, half, mat)
        b_copy(0, 0, y, 1 - core).wait_recv()

    for slot in (1, 2, 3):
        for mat in range(2):
            w_get(slot, 1 - core, mat)
        b_copy(slot, 0, y, 1 - core).wait_recv()

    for j in range(4):
        if j:
            get_along(s2_copy, j)
        cols = cols_of(j)
        for slot in range(4):
            H[slot] = (H[slot] if j else 0.0) + jnp.dot(R2[:, cols], W[slot, cols], preferred_element_type=F32)

    for slot in range(4):
        back = BK[slot, 0:1]

        for i in range(nz // 2):
            at = pl.ds(i * 4 * group, 4 * group)
            gate_side, up_side = H[slot, at, 0:ff], H[slot, at, ff:]
            gate_out, up_out = [], []
            for s in range(2):
                lo = 2 * s * group
                h, dh = gate_side[lo : lo + group], gate_side[lo + group : lo + 2 * group]
                u, du = up_side[lo : lo + group], up_side[lo + group : lo + 2 * group]
                sig = jax.nn.sigmoid(h)
                first = sig * (1.0 + h * (1.0 - sig))
                second = sig * (1.0 - sig) * (2.0 + h * (1.0 - 2.0 * sig))
                gate_out.append(back * (du * first + u * second * dh))
                up_out.append(back * first * dh)
            to = pl.ds(i * 2 * group, 2 * group)
            C[slot, to, 0:ff] = jnp.concatenate(gate_out, 0).astype(BF16)
            C[slot, to, ff:] = jnp.concatenate(up_out, 0).astype(BF16)

    def product(n, cols):
        lo, hi = cols
        total = 0.0
        for slot in range(4):
            total = total + lax.dot_general(
                C[slot], W[slot, pl.ds(n * qw + lo, hi - lo)], NT, preferred_element_type=F32
            )
        return total

    for j in range(4):
        sent_near(s1_copy, j)

    short = (qw // 128 * 2 // 7 or 1) * 128
    spans = [[(0, short), (short, qw)], [(0, qw - short), (qw - short, qw)]]
    if short == qw:
        spans = [[(0, qw // 2), (qw // 2, qw)]] * 2

    def span(c, i):
        lo, hi = spans[c][i]
        return pl.ds(lo, hi - lo)

    def q1_piece(c, i):
        def q1_copy(_, to, slot):
            return remote(
                S1.at[c, rows_at(to, m2), span(c, i)], Q1.at[c, rows_at(slot, m2), span(c, i)],
                q1_send.at[c, i, to], q1_recv.at[c, i, slot], along(to),
            )

        return q1_copy

    def q2_copy(c, to, slot):
        return remote(
            S1.at[2 + c, rows_at(to, m1)], Q2.at[c, rows_at(slot, m1)],
            q2_send.at[c, to], q2_recv.at[c, slot], near(to),
        )

    def go_along(c, i):
        send_along(q1_piece(c, i), c)
        Q1[c, rows_at(z, m2), span(c, i)] = S1[c, rows_at(z, m2), span(c, i)]

    def go_near(c, rows):
        S1[2 + c] = mix(to_d_ref[...], rows)
        send_near(q2_copy, c)
        Q2[c, rows_at(d, m1)] = S1[2 + c, rows_at(d, m1)]

    def r_piece(c, i, slot, to):
        def r_copy():
            return remote(
                PTB.at[to, :, span(c, i)], RS.at[slot, :, span(c, i)],
                r_send.at[slot, i], r_recv.at[slot, i], across(to),
            )

        return r_copy()

    def combine(c, i, rows):
        summed = jnp.dot(CB[c], rows, preferred_element_type=F32)
        for half in range(2):
            lo = 2 * half * toks
            full = summed[lo : lo + toks] + summed[lo + toks : lo + 2 * toks]
            PTF[2 * half + c, :, span(c, i)] = full
            PTB[2 * half + c, :, span(c, i)] = full.astype(BF16)
        for slot, to in enumerate(others):
            @pl.when(lax.rem(to, 2) == c)
            def _():
                r_piece(c, i, slot, to).start()

    for c in range(2):
        for i in range(2):
            for half in range(2):
                A[half, :, span(c, i)] = product(2 * half + c, spans[c][i])

            @pl.loop(0, nz)
            def _(k):
                at = rows_at(k, group)
                both = jnp.concatenate([A[0, at, span(c, i)], A[1, at, span(c, i)]], 0)
                S1[c, rows_at(k, m2), span(c, i)] = both.astype(BF16)

            if c == 0:
                go_along(0, i)
    go_near(1, S1[1])
    get_near(q2_copy, 1)
    S1[1] = mix(to_z_ref[...], Q2[1])
    for i in range(2):
        go_along(1, i)
    for i in range(2):
        get_along(q1_piece(0, i), 0)
    go_near(0, Q1[0])
    get_near(q2_copy, 0)
    for i in range(2):
        combine(0, i, Q2[0, :, span(0, i)])
    for i in range(2):
        get_along(q1_piece(1, i), 1)
        combine(1, i, Q1[1, :, span(1, i)])

    for c in range(2):
        @pl.when(odd == c)
        def _():
            for i in range(2):
                total = PTF[y, :, span(c, i)]
                for slot, to in enumerate(others):
                    r_got = r_piece(c, i, slot, y)
                    r_got.wait_recv()
                    total = total + RS[slot, :, span(c, i)].astype(F32)
                out_ref[:, span(c, i)] = total.astype(BF16)

    for slot, to in enumerate(others):
        for c in range(2):
            @pl.when(lax.rem(to, 2) == c)
            def _():
                for i in range(2):
                    r_piece(c, i, slot, to).wait_send()

    for slot in (1, 2):
        for kind in range(2):
            t_own(slot, kind).wait_send()
    t_on().wait_send()

    @pl.when(home)
    def _():
        for half, mat in pieces:
            w_from(1, half, mat, mate, half, 0).wait_send()
            w_from(0, half, mat, y, 1 - core, 1).wait_send()
        for c in b_home():
            c.wait_send()

    @pl.when(away)
    def _():
        for half, mat in pieces:
            w_from(2, half, mat, outer, half, 0).wait_send()
        for c in b_away():
            c.wait_send()

    for mat in range(2):
        for slot in (1, 2, 3):
            w_on(slot, core, mat, slot, y, 1 - core, slot + 1).wait_send()
        w_on(2, core, mat, 3, mate, core, 5).wait_send()
    for j in range(4):
        sent_along(s2_copy, j)
    for c in range(2):
        for i in range(2):
            sent_along(q1_piece(c, i), c)
        sent_near(q2_copy, c)


def shards(near, tokens, tangents, routes, gates, gate_weight, up_weight, down_weight, readout):
    experts, parts = lax.axis_size("expert"), lax.axis_size("tensor")
    toks, qw = tokens.shape
    depth, ff = gate_weight.shape[1:]
    most = toks * routes.shape[1] * 5 // (4 * experts)
    share = most // parts
    nd, nz = near, experts // near
    rows = experts * share * 2
    expand, target, to_z, to_d, expand_back, target_back = tables(nz, nd, share, parts)
    hbm, vmem = pl.BlockSpec(memory_space=pl.ANY), pl.BlockSpec(memory_space=pltpu.VMEM)
    dma = pltpu.SemaphoreType.DMA
    return pl.pallas_call(
        functools.partial(kernel, (nz, nd, share, parts)),
        out_shape=jax.ShapeDtypeStruct((toks, qw), BF16),
        in_specs=[hbm] * 5 + [vmem] * 5 + [hbm] * 2 + [vmem] * 2,
        out_specs=vmem,
        scratch_shapes=[
            pltpu.VMEM((4, 2 * toks, qw), BF16),
            pltpu.VMEM((4, rows, qw), BF16),
            pltpu.VMEM((4, rows, qw), BF16),
            pltpu.VMEM((4, rows, qw), BF16),
            pltpu.VMEM((rows, depth), BF16),
            pltpu.VMEM((4, depth, 2 * ff), BF16),
            pltpu.VMEM((4, rows, 2 * ff), F32),
            pltpu.VMEM((4, rows // 2, 2 * ff), BF16),
            pltpu.VMEM((2, rows // 2, qw), F32),
            pltpu.VMEM((2, rows, qw), BF16),
            pltpu.VMEM((2, rows, qw), BF16),
            pltpu.VMEM((ff, depth), BF16),
            pltpu.VMEM((8, ff), F32),
            pltpu.VMEM((4, 8, ff), F32),
            pltpu.VMEM((4, toks, qw), F32),
            pltpu.VMEM((4, toks, qw), BF16),
            pltpu.VMEM((3, toks, qw), BF16),
            pltpu.VMEM((rows, qw), BF16),
            pltpu.VMEM((rows, 2 * toks), BF16),
            pltpu.VMEM((rows, 2 * toks), BF16),
            pltpu.VMEM((2, 4 * toks, rows), BF16),
            pltpu.VMEM((rows, rows), BF16),
            pltpu.VMEM((rows, rows), BF16),
            dma((7,)),
            dma((4, 2)), dma((4, 2)),
            dma((6, 2, 2)), dma((4, 2, 2)),
            dma((4,)), dma((4,)),
            dma((4, nd)), dma((4, nd)),
            dma((4, nz)), dma((4, nz)),
            dma((2, 2, nz)), dma((2, 2, nz)),
            dma((2, nd)), dma((2, nd)),
            dma((3, 2)), dma((3, 2)),
        ],
        compiler_params=pltpu.CompilerParams(
            collective_id=0, has_side_effects=True, vmem_limit_bytes=62 * 2**20
        ),
    )(
        tokens, tangents, gate_weight, up_weight, down_weight,
        routes.T, gates.T, readout,
        jnp.asarray(expand, BF16), jnp.asarray(target, F32), jnp.asarray(to_z, BF16),
        jnp.asarray(to_d, BF16), jnp.asarray(expand_back, BF16), jnp.asarray(target_back, F32),
    )


def solution(mesh):
    return jax.shard_map(
        functools.partial(shards, NEAR),
        mesh=mesh,
        in_specs=(
            P("expert", "tensor"),
            P("expert", "tensor"),
            P("expert", None),
            P("expert", None),
            P("expert", None, "tensor"),
            P("expert", None, "tensor"),
            P("expert", "tensor", None),
            P(),
        ),
        out_specs=P("expert", "tensor"),
        check_vma=False,
    )
```

```python
import functools

import jax
import jax.numpy as jnp
import numpy as np
from jax import lax
from jax.experimental import pallas as pl
from jax.experimental.pallas import tpu as pltpu
from jax.sharding import PartitionSpec as P

MESH = pl.DeviceIdType.MESH
NEAR = 8
F32 = jnp.float32
BF16 = jnp.bfloat16
NT = (((1,), (1,)), ((), ()))


def tables(nz, nd, share, parts):
    rows = nz * nd * 2 * share
    experts = nz * nd
    expand = np.zeros((2, rows, experts), np.float32)
    target = np.full((rows, 2), -100.0, np.float32)
    to_z = np.zeros((rows, rows), np.float32)
    expand_back = np.zeros((2, experts, rows), np.float32)
    target_back = np.full((8, rows), -100.0, np.float32)
    for z in range(nz):
        for d in range(nd):
            for k in range(2):
                for q in range(share):
                    by_z = ((z * 2 + k) * nd + d) * share + q
                    by_d = ((d * 2 + k) * nz + z) * share + q
                    for own in range(2):
                        e = z * nd + d // 2 * 2 + own
                        expand[own, by_z, e] = 1
                        expand_back[own, e, by_d] = 1
                    target[by_z, k] = parts * q + d % 2
                    target_back[k, by_d] = parts * q + d % 2
                    to_z[by_z, by_d] = 1
    return expand, target, to_z, to_z.T, expand_back, target_back


def kernel(
    dims,
    tok_ref, tan_ref, gw_ref, uw_ref, dw_ref,
    routes_ref, gates_ref, readout_ref,
    expand_ref, target_ref, to_z_hbm, to_d_hbm, expand_back_ref, target_back_ref,
    out_ref,
    T, S1, R1, S2, R2, W, H, C, A, Q1, Q2, DW, BO, BK, PTF, PTB, RS, X0, PZ, PD, CB, to_z_ref, to_d_ref,
    local_sem, t_send, t_recv, w_send, w_recv, b_send, b_recv,
    s1_send, s1_recv, s2_send, s2_recv, q1_send, q1_recv, q2_send, q2_recv, r_send, r_recv,
):
    nz, nd, share, parts = dims
    toks, qw = tok_ref.shape
    depth, ff = gw_ref.shape[1:]
    half_depth = depth // 2
    experts = nz * nd
    m1, m2 = nz * 2 * share, nd * 2 * share
    group = nd * share
    me, y = lax.axis_index("expert"), lax.axis_index("tensor")
    z, d = me // nd, lax.rem(me, nd)
    own, odd, core = y // 2, lax.rem(y, 2), lax.rem(me, 2)
    home = core == own
    away = core != own
    mate, outer, far = y + 1 - 2 * odd, parts - 1 - y, lax.rem(y + 2, parts)
    others = (mate, outer, far)

    def near(dd):
        return (z * nd + dd, y)

    def along(zz):
        return (zz * nd + d, y)

    def across(yy, cc=None):
        return (me if cc is None else me - core + cc, yy)

    def rows_at(i, n):
        return pl.ds(pl.multiple_of(i * n, n), n)

    def remote(src, dst, ss, rs, dev):
        return pltpu.make_async_remote_copy(
            src_ref=src, dst_ref=dst, send_sem=ss, recv_sem=rs, device_id=dev, device_id_type=MESH
        )

    barrier = pltpu.get_barrier_semaphore()
    for yy in others:
        for cc in range(2):
            pl.semaphore_signal(barrier, inc=1, device_id=across(yy, cc), device_id_type=MESH)

    @pl.loop(1, nd)
    def _(k):
        pl.semaphore_signal(barrier, inc=1, device_id=near(lax.rem(d + k, nd)), device_id_type=MESH)

    @pl.loop(1, nz)
    def _(k):
        pl.semaphore_signal(barrier, inc=1, device_id=along(lax.rem(z + k, nz)), device_id_type=MESH)

    local = [
        pltpu.make_async_copy(tok_ref, T.at[0, pl.ds(0, toks)], local_sem.at[0]),
        pltpu.make_async_copy(tan_ref, T.at[0, pl.ds(toks, toks)], local_sem.at[1]),
        pltpu.make_async_copy(dw_ref.at[0], DW, local_sem.at[2]),
        pltpu.make_async_copy(to_d_hbm, to_d_ref, local_sem.at[5]),
        pltpu.make_async_copy(to_z_hbm, to_z_ref, local_sem.at[6]),
    ]
    stage = [
        pltpu.make_async_copy(gw_ref.at[0], W.at[0, :, pl.ds(0, ff)], local_sem.at[3]),
        pltpu.make_async_copy(uw_ref.at[0], W.at[0, :, pl.ds(ff, ff)], local_sem.at[4]),
    ]
    for c in local:
        c.start()

    @pl.when(home)
    def _():
        for c in stage:
            c.start()

    def t_own(slot, kind):
        return remote(
            (tok_ref, tan_ref)[kind], T.at[slot, pl.ds(kind * toks, toks)],
            t_send.at[slot, kind], t_recv.at[slot, kind], across(others[slot - 1]),
        )

    def t_on():
        return remote(T.at[1], T.at[3], t_send.at[3, 0], t_recv.at[3, 0], across(outer))

    def w_from(slot, half, mat, yy, cc, sem):
        part = pl.ds(half * half_depth, half_depth)
        return remote(
            (gw_ref, uw_ref)[mat].at[0, part], W.at[slot, part, pl.ds(mat * ff, ff)],
            w_send.at[sem, half, mat], w_recv.at[slot, half, mat], across(yy, cc),
        )

    def w_on(slot, half, mat, slot_to, yy, cc, sem):
        part, cols = pl.ds(pl.multiple_of(half * half_depth, half_depth), half_depth), pl.ds(mat * ff, ff)
        return remote(
            W.at[slot, part, cols], W.at[slot_to, part, cols],
            w_send.at[sem, half, mat], w_recv.at[slot_to, half, mat], across(yy, cc),
        )

    pieces = [(half, mat) for mat in range(2) for half in range(2)]

    def w_get(slot, half, mat):
        w_on(slot, half, mat, slot, y, 1 - core, slot + 1).wait_recv()

    def pass_on(slot, mat):
        w_get(slot, core, mat)
        w_on(slot, core, mat, slot, y, 1 - core, slot + 1).start()
        if slot == 2:
            w_on(2, core, mat, 3, mate, core, 5).start()

    top = routes_ref.shape[0]
    ids = lax.broadcasted_iota(jnp.int32, (experts, toks), 0)
    chosen = jnp.zeros((experts, toks), F32)
    for k in range(top):
        chosen = jnp.where(routes_ref[pl.ds(k, 1), :] == ids, 1.0, chosen)
    earlier = (
        lax.broadcasted_iota(jnp.int32, (toks, toks), 0) < lax.broadcasted_iota(jnp.int32, (toks, toks), 1)
    ).astype(F32).astype(BF16)
    place = jnp.dot(chosen.astype(BF16), earlier, preferred_element_type=F32)
    taken = jnp.where(chosen > 0.5, place, -1.0).astype(BF16)
    mine = (2 * odd).astype(F32)
    place = jnp.dot(expand_ref[own], taken, preferred_element_type=F32) - mine
    for kind in range(2):
        hit = place == target_ref[:, pl.ds(kind, 1)]
        PZ[:, pl.ds(kind * toks, toks)] = jnp.where(hit, 1.0, 0.0).astype(BF16)

    def owner(j):
        return (y, mate, outer, far)[j]

    def cols_of(j):
        return pl.ds(pl.multiple_of(owner(j) * qw, qw), qw)

    def s1_copy(j, to, slot):
        at = rows_at(slot, m1)
        return remote(
            S1.at[j, rows_at(to, m1)], R1.at[j, at] if j > 1 else X0.at[j, at],
            s1_send.at[j, to], s1_recv.at[j, slot], near(to),
        )

    def s2_copy(j, to, slot):
        at = rows_at(slot, m2)
        return remote(
            S2.at[j, rows_at(to, m2)], R2.at[at, cols_of(j)] if j > 1 else R1.at[j, at],
            s2_send.at[j, to], s2_recv.at[j, slot], along(to),
        )

    def send_near(copy, j):
        @pl.loop(1, nd)
        def _(k):
            copy(j, lax.rem(d + k, nd), d).start()

    def send_along(copy, j):
        @pl.loop(1, nz)
        def _(k):
            copy(j, lax.rem(z + k, nz), z).start()

    def get_near(copy, j):
        @pl.loop(1, nd)
        def _(k):
            s = lax.rem(d + nd - k, nd)
            copy(j, s, s).wait_recv()

    def get_along(copy, j):
        @pl.loop(1, nz)
        def _(k):
            s = lax.rem(z + nz - k, nz)
            copy(j, s, s).wait_recv()

    def sent_near(copy, j):
        @pl.loop(1, nd)
        def _(k):
            copy(j, lax.rem(d + k, nd), d).wait_send()

    def sent_along(copy, j):
        @pl.loop(1, nz)
        def _(k):
            copy(j, lax.rem(z + k, nz), z).wait_send()

    def mix(table, rows):
        return jnp.dot(table, rows, preferred_element_type=F32).astype(BF16)

    def pack(j):
        S1[j] = mix(PD[...], T[j])
        send_near(s1_copy, j)
        R1[j, rows_at(d, m1)] = S1[j, rows_at(d, m1)]

    def first(j):
        S2[j] = mix(PZ[...], T[j])

    def leave(j):
        send_along(s2_copy, j)
        R1[j, rows_at(z, m2)] = S2[j, rows_at(z, m2)]

    def flip(j):
        get_along(s2_copy, j)
        S1[j] = mix(to_d_ref[...], R1[j])
        send_near(s1_copy, j)
        X0[j, rows_at(d, m1)] = S1[j, rows_at(d, m1)]

    def finish(j):
        get_near(s1_copy, j)
        R2[:, cols_of(j)] = mix(to_z_ref[...], X0[j])

    def turn(j):
        get_near(s1_copy, j)
        S2[j] = mix(to_z_ref[...], R1[j])
        send_along(s2_copy, j)
        R2[rows_at(z, m2), cols_of(j)] = S2[j, rows_at(z, m2)]

    local[0].wait()
    local[1].wait()
    first(0)
    pl.semaphore_wait(barrier, 2 * 3 + nd - 1 + nz - 1)
    leave(0)
    for slot in (1, 2):
        for kind in range(2):
            t_own(slot, kind).start()

    @pl.when(home)
    def _():
        for half, mat in pieces:
            w_from(1, half, mat, mate, half, 0).start()
        for half, mat in pieces:
            w_from(0, half, mat, y, 1 - core, 1).start()

    @pl.when(away)
    def _():
        for half, mat in pieces:
            w_from(2, half, mat, outer, half, 0).start()

    local[3].wait()
    local[4].wait()
    PD[...] = mix(to_d_ref[...], PZ[...])

    local[2].wait()
    vec = jnp.broadcast_to(readout_ref[...][None, :], (16, depth))
    BO[...] = lax.dot_general(vec, DW[...], NT, preferred_element_type=F32)[0:8]

    def b_copy(slot, i, yy, cc):
        return remote(BO, BK.at[slot], b_send.at[i], b_recv.at[slot], across(yy, cc))

    def b_home():
        return [b_copy(0, 0, y, 1 - core), b_copy(1, 1, mate, 0), b_copy(1, 2, mate, 1)]

    def b_away():
        return [b_copy(slot, 2 * slot - 4 + cc, yy, cc) for slot, yy in ((2, outer), (3, far)) for cc in range(2)]

    @pl.when(home)
    def _():
        for c in b_home():
            c.start()
        BK[0] = BO[...]

    @pl.when(away)
    def _():
        for c in b_away():
            c.start()

    for kind in range(2):
        t_own(1, kind).wait_recv()
    t_on().start()
    first(1)
    leave(1)
    for kind in range(2):
        t_own(2, kind).wait_recv()
    pack(2)
    flip(0)
    turn(2)
    pass_on(2, 0)
    t_on().wait_recv()
    pack(3)
    pass_on(2, 1)
    pass_on(1, 0)
    turn(3)
    flip(1)
    pass_on(1, 1)

    gate = jnp.zeros((experts, toks), F32)
    for k in range(top):
        gate = jnp.where(routes_ref[pl.ds(k, 1), :] == ids, gates_ref[pl.ds(k, 1), :], gate)
    high = gate.astype(BF16)
    low = (gate - high.astype(F32)).astype(BF16)
    place, high, low = [
        lax.dot_general(a, expand_back_ref[own], (((0,), (0,)), ((), ())), preferred_element_type=F32)
        for a in (taken, high, low)
    ]
    place = place - mine
    for half in range(2):
        hit = place == target_back_ref[pl.ds(half, 1), :]
        CB[0, pl.ds(2 * half * toks, toks)] = jnp.where(hit, high, 0.0).astype(BF16)
        CB[0, pl.ds((2 * half + 1) * toks, toks)] = jnp.where(hit, low, 0.0).astype(BF16)
    CB[1] = mix(CB[0], to_d_ref[...])

    finish(0)

    pass_on(3, 0)
    pass_on(3, 1)

    @pl.when(home)
    def _():
        for c in stage:
            c.wait()

    @pl.when(away)
    def _():
        for half, mat in pieces:
            w_get(0, half, mat)
        b_copy(0, 0, y, 1 - core).wait_recv()

    for slot in (1, 2, 3):
        for mat in range(2):
            w_get(slot, 1 - core, mat)
        b_copy(slot, 0, y, 1 - core).wait_recv()

    for j in range(4):
        if j > 1:
            get_along(s2_copy, j)
        elif j == 1:
            finish(1)
        cols = cols_of(j)
        for slot in range(4):
            H[slot] = (H[slot] if j else 0.0) + jnp.dot(R2[:, cols], W[slot, cols], preferred_element_type=F32)

    for slot in range(4):
        back = BK[slot, 0:1]

        for i in range(nz // 2):
            at = pl.ds(i * 4 * group, 4 * group)
            gate_side, up_side = H[slot, at, 0:ff], H[slot, at, ff:]
            gate_out, up_out = [], []
            for s in range(2):
                lo = 2 * s * group
                h, dh = gate_side[lo : lo + group], gate_side[lo + group : lo + 2 * group]
                u, du = up_side[lo : lo + group], up_side[lo + group : lo + 2 * group]
                sig = jax.nn.sigmoid(h)
                first = sig * (1.0 + h * (1.0 - sig))
                second = sig * (1.0 - sig) * (2.0 + h * (1.0 - 2.0 * sig))
                gate_out.append(back * (du * first + u * second * dh))
                up_out.append(back * first * dh)
            to = pl.ds(i * 2 * group, 2 * group)
            C[slot, to, 0:ff] = jnp.concatenate(gate_out, 0).astype(BF16)
            C[slot, to, ff:] = jnp.concatenate(up_out, 0).astype(BF16)

    def product(n, cols):
        lo, hi = cols
        total = 0.0
        for slot in range(4):
            total = total + lax.dot_general(
                C[slot], W[slot, pl.ds(n * qw + lo, hi - lo)], NT, preferred_element_type=F32
            )
        return total

    for j in range(4):
        sent_near(s1_copy, j)

    short = (qw // 128 * 2 // 7 or 1) * 128
    spans = [[(0, short), (short, qw)], [(0, qw - short), (qw - short, qw)]]
    if short == qw:
        spans = [[(0, qw // 2), (qw // 2, qw)]] * 2

    def span(c, i):
        lo, hi = spans[c][i]
        return pl.ds(lo, hi - lo)

    def q1_piece(c, i):
        def q1_copy(_, to, slot):
            return remote(
                S1.at[c, rows_at(to, m2), span(c, i)], Q1.at[c, rows_at(slot, m2), span(c, i)],
                q1_send.at[c, i, to], q1_recv.at[c, i, slot], along(to),
            )

        return q1_copy

    def q2_copy(c, to, slot):
        return remote(
            S1.at[2 + c, rows_at(to, m1)], Q2.at[c, rows_at(slot, m1)],
            q2_send.at[c, to], q2_recv.at[c, slot], near(to),
        )

    def go_along(c, i):
        send_along(q1_piece(c, i), c)
        Q1[c, rows_at(z, m2), span(c, i)] = S1[c, rows_at(z, m2), span(c, i)]

    def go_near(c, rows):
        S1[2 + c] = mix(to_d_ref[...], rows)
        send_near(q2_copy, c)
        Q2[c, rows_at(d, m1)] = S1[2 + c, rows_at(d, m1)]

    def r_piece(c, i, slot, to):
        def r_copy():
            return remote(
                PTB.at[to, :, span(c, i)], RS.at[slot, :, span(c, i)],
                r_send.at[slot, i], r_recv.at[slot, i], across(to),
            )

        return r_copy()

    def combine(c, i, rows):
        summed = jnp.dot(CB[c], rows, preferred_element_type=F32)
        for half in range(2):
            lo = 2 * half * toks
            full = summed[lo : lo + toks] + summed[lo + toks : lo + 2 * toks]
            PTF[2 * half + c, :, span(c, i)] = full
            PTB[2 * half + c, :, span(c, i)] = full.astype(BF16)
        for slot, to in enumerate(others):
            @pl.when(lax.rem(to, 2) == c)
            def _():
                r_piece(c, i, slot, to).start()

    for c in range(2):
        for i in range(2):
            for half in range(2):
                A[half, :, span(c, i)] = product(2 * half + c, spans[c][i])

            @pl.loop(0, nz)
            def _(k):
                at = rows_at(k, group)
                both = jnp.concatenate([A[0, at, span(c, i)], A[1, at, span(c, i)]], 0)
                S1[c, rows_at(k, m2), span(c, i)] = both.astype(BF16)

            if c == 0:
                go_along(0, i)
    go_near(1, S1[1])
    get_near(q2_copy, 1)
    S1[1] = mix(to_z_ref[...], Q2[1])
    for i in range(2):
        go_along(1, i)
    for i in range(2):
        get_along(q1_piece(0, i), 0)
    go_near(0, Q1[0])
    get_near(q2_copy, 0)
    for i in range(2):
        combine(0, i, Q2[0, :, span(0, i)])
    for i in range(2):
        get_along(q1_piece(1, i), 1)
        combine(1, i, Q1[1, :, span(1, i)])

    for c in range(2):
        @pl.when(odd == c)
        def _():
            for i in range(2):
                total = PTF[y, :, span(c, i)]
                for slot, to in enumerate(others):
                    r_got = r_piece(c, i, slot, y)
                    r_got.wait_recv()
                    total = total + RS[slot, :, span(c, i)].astype(F32)
                out_ref[:, span(c, i)] = total.astype(BF16)

    for slot, to in enumerate(others):
        for c in range(2):
            @pl.when(lax.rem(to, 2) == c)
            def _():
                for i in range(2):
                    r_piece(c, i, slot, to).wait_send()

    for slot in (1, 2):
        for kind in range(2):
            t_own(slot, kind).wait_send()
    t_on().wait_send()

    @pl.when(home)
    def _():
        for half, mat in pieces:
            w_from(1, half, mat, mate, half, 0).wait_send()
            w_from(0, half, mat, y, 1 - core, 1).wait_send()
        for c in b_home():
            c.wait_send()

    @pl.when(away)
    def _():
        for half, mat in pieces:
            w_from(2, half, mat, outer, half, 0).wait_send()
        for c in b_away():
            c.wait_send()

    for mat in range(2):
        for slot in (1, 2, 3):
            w_on(slot, core, mat, slot, y, 1 - core, slot + 1).wait_send()
        w_on(2, core, mat, 3, mate, core, 5).wait_send()
    for j in range(4):
        sent_along(s2_copy, j)
    for c in range(2):
        for i in range(2):
            sent_along(q1_piece(c, i), c)
        sent_near(q2_copy, c)


def shards(near, tokens, tangents, routes, gates, gate_weight, up_weight, down_weight, readout):
    experts, parts = lax.axis_size("expert"), lax.axis_size("tensor")
    toks, qw = tokens.shape
    depth, ff = gate_weight.shape[1:]
    most = toks * routes.shape[1] * 5 // (4 * experts)
    share = most // parts
    nd, nz = near, experts // near
    rows = experts * share * 2
    expand, target, to_z, to_d, expand_back, target_back = tables(nz, nd, share, parts)
    hbm, vmem = pl.BlockSpec(memory_space=pl.ANY), pl.BlockSpec(memory_space=pltpu.VMEM)
    dma = pltpu.SemaphoreType.DMA
    return pl.pallas_call(
        functools.partial(kernel, (nz, nd, share, parts)),
        out_shape=jax.ShapeDtypeStruct((toks, qw), BF16),
        in_specs=[hbm] * 5 + [vmem] * 5 + [hbm] * 2 + [vmem] * 2,
        out_specs=vmem,
        scratch_shapes=[
            pltpu.VMEM((4, 2 * toks, qw), BF16),
            pltpu.VMEM((4, rows, qw), BF16),
            pltpu.VMEM((4, rows, qw), BF16),
            pltpu.VMEM((4, rows, qw), BF16),
            pltpu.VMEM((rows, depth), BF16),
            pltpu.VMEM((4, depth, 2 * ff), BF16),
            pltpu.VMEM((4, rows, 2 * ff), F32),
            pltpu.VMEM((4, rows // 2, 2 * ff), BF16),
            pltpu.VMEM((2, rows // 2, qw), F32),
            pltpu.VMEM((2, rows, qw), BF16),
            pltpu.VMEM((2, rows, qw), BF16),
            pltpu.VMEM((ff, depth), BF16),
            pltpu.VMEM((8, ff), F32),
            pltpu.VMEM((4, 8, ff), F32),
            pltpu.VMEM((4, toks, qw), F32),
            pltpu.VMEM((4, toks, qw), BF16),
            pltpu.VMEM((3, toks, qw), BF16),
            pltpu.VMEM((2, rows, qw), BF16),
            pltpu.VMEM((rows, 2 * toks), BF16),
            pltpu.VMEM((rows, 2 * toks), BF16),
            pltpu.VMEM((2, 4 * toks, rows), BF16),
            pltpu.VMEM((rows, rows), BF16),
            pltpu.VMEM((rows, rows), BF16),
            dma((7,)),
            dma((4, 2)), dma((4, 2)),
            dma((6, 2, 2)), dma((4, 2, 2)),
            dma((4,)), dma((4,)),
            dma((4, nd)), dma((4, nd)),
            dma((4, nz)), dma((4, nz)),
            dma((2, 2, nz)), dma((2, 2, nz)),
            dma((2, nd)), dma((2, nd)),
            dma((3, 2)), dma((3, 2)),
        ],
        compiler_params=pltpu.CompilerParams(
            collective_id=0, has_side_effects=True, vmem_limit_bytes=62 * 2**20
        ),
    )(
        tokens, tangents, gate_weight, up_weight, down_weight,
        routes.T, gates.T, readout,
        jnp.asarray(expand, BF16), jnp.asarray(target, F32), jnp.asarray(to_z, BF16),
        jnp.asarray(to_d, BF16), jnp.asarray(expand_back, BF16), jnp.asarray(target_back, F32),
    )


def solution(mesh):
    return jax.shard_map(
        functools.partial(shards, NEAR),
        mesh=mesh,
        in_specs=(
            P("expert", "tensor"),
            P("expert", "tensor"),
            P("expert", None),
            P("expert", None),
            P("expert", None, "tensor"),
            P("expert", None, "tensor"),
            P("expert", "tensor", None),
            P(),
        ),
        out_specs=P("expert", "tensor"),
        check_vma=False,
    )
```
